128 devices in a mesh: dp: 8 (over z_lo, x), fsdp: 16 (over z_hi, y, core).
Axes of the slice: x: 4, y: 4, z: 4 (z_hi: 2, z_lo: 2; z = z_hi * 2 + z_lo), core: 2. Of those that a mesh axis runs over, the one named last changes fastest.
Arguments:
- activations: bfloat16 [65536, 8192], P('dp', 'fsdp'), may hold values from -6 to 6
- grad_out: bfloat16 [65536, 1024], P(('dp', 'fsdp')), may hold values from -3 to 3
- base_weight: bfloat16 [8192, 1024], P('fsdp'), may hold values from -0.1875 to 0.1875
- down_param: float32 [16, 8192, 64], P('dp', 'fsdp'), may hold values from -0.0625 to 0.0625
- up_param: float32 [16, 64, 1024], P('dp', None, 'fsdp'), may hold values from -0.1875 to 0.1875
- down_first: float32 [16, 8192, 64], P('dp', 'fsdp'), may hold values from -3 to 3
- down_second: float32 [16, 8192, 64], P('dp', 'fsdp'), may hold values from 0.01 to 1
- up_first: float32 [16, 64, 1024], P('dp', None, 'fsdp'), may hold values from -3 to 3
- up_second: float32 [16, 64, 1024], P('dp', None, 'fsdp'), may hold values from 0.01 to 1
- counts: int32 [16], replicated, may hold values from 1 to 7936, 63488 in all
- slot_language: int32 [16], replicated, may hold values from 0 to 15, each once
Outputs:
- input_gradient: bfloat16 [65536, 8192], P('dp', 'fsdp')
- new_down: float32 [16, 8192, 64], P('dp', 'fsdp')
- new_up: float32 [16, 64, 1024], P('dp', None, 'fsdp')
- new_down_first: float32 [16, 8192, 64], P('dp', 'fsdp')
- new_down_second: float32 [16, 8192, 64], P('dp', 'fsdp')
- new_up_first: float32 [16, 64, 1024], P('dp', None, 'fsdp')
- new_up_second: float32 [16, 64, 1024], P('dp', None, 'fsdp')
The draws below stay inside these ranges and needn't reach their ends.
Inputs may be any that keep to these rules, and one draw needn't show every extreme that they name: Every language has at least one token; the counts sum to (64 * 8 - 16) * 128 and the largest is exactly that over 8. `slot_language`: a permutation: each language in exactly one slot.
All inputs are finite; a program needn't handle non-finite values.
Results may differ from the reference program's by a relative error of at most 0.0055.
Values may be sent and summed in bfloat16 or wider, within the bound.
A program may use at most 128 MiB of HBM per device.

```python
import math
import jax
import jax.numpy as jnp
import numpy as np
from jax import lax

D = 8192
KV = 1024
R = 64
LANGS = 16
BLK = 128
STEP = 100
BLOCKS_DP = 64
ROWS = 65536
N_DP = 8


def block_levels(own_key, dims, cuts, least, largest):
    gain, own = 1.0, jax.random.fold_in(own_key, 6)
    for dim, parts in cuts:
        draws = jnp.exp(jax.random.uniform(jax.random.fold_in(own, dim), (parts,), jnp.float32, least / len(cuts), largest / len(cuts)))
        gain = gain * jnp.repeat(draws, dims[dim] // parts).reshape([-1 if axis == dim else 1 for axis in range(len(dims))])
    return gain


def split_up(count, total, reach, slope):
    weights = [(1 << 20) // math.isqrt(grade ** slope) + 1 for grade in range(2, count + 1)]
    surplus, given = total - reach - (count - 1), [1] * (count - 1)
    while surplus > 0:
        free = [i for i in range(count - 1) if given[i] < reach]
        whole, budget = sum([weights[i] for i in free]), surplus
        for i in free:
            more = min(reach - given[i], max(1, budget * weights[i] // whole), surplus)
            given[i] = given[i] + more
            surplus = surplus - more
    return np.array([reach] + given)


def uneven(own_key, count, total, most, skew):
    if count == 2:
        one = jax.random.randint(own_key, (), max(1, total - most), min(most, total - 1) + 1)
        return jnp.stack([one, total - one])
    sizes = jnp.asarray(split_up(count, total, most, skew), jnp.int32)
    twos = (count - 1) // 2
    giver, taker = sizes[1:1 + 2 * twos:2], sizes[2:2 + 2 * twos:2]
    room = jnp.minimum(giver - 1, most - taker)
    passed = jax.random.randint(jax.random.fold_in(own_key, 1), (twos,), 0, 1 << 20) % (room + 1)
    sizes = sizes.at[1:1 + 2 * twos:2].set(giver - passed).at[2:2 + 2 * twos:2].set(taker + passed)
    return sizes[jax.random.permutation(jax.random.fold_in(own_key, 2), count)]


def scatter_about(key, dims, scale, limit, cuts=(), kind=jnp.bfloat16):
    values = scale * jax.random.normal(key, dims, jnp.float32)
    if cuts:
        values = values * block_levels(key, dims, cuts, -0.22, 0.18)
    return jnp.clip(values, -limit, limit).astype(kind)


def setup_inputs(seed: int = 0) -> dict:
    splits = jax.random.split(jax.random.key(seed), 12)
    return {
        "activations": scatter_about(splits[0], (ROWS, D), 1.0, 6.0, ((0, 8), (1, 16))),
        "grad_out": scatter_about(splits[1], (ROWS, KV), 0.5, 3.0, ((0, 128),)),
        "base_weight": scatter_about(splits[2], (D, KV), KV ** -0.5, 0.1875, ((0, 16),)),
        "down_param": scatter_about(splits[3], (LANGS, D, R), D ** -0.5, 0.0625, ((0, 8), (1, 16)), jnp.float32),
        "up_param": scatter_about(splits[4], (LANGS, R, KV), KV ** -0.5, 0.1875, ((0, 8), (2, 16)), jnp.float32),
        "down_first": scatter_about(splits[5], (LANGS, D, R), 0.5, 3.0, ((0, 8), (1, 16)), jnp.float32),
        "down_second": jnp.clip(jnp.exp(math.log(1.0) - 4.6051702 * jax.random.uniform(splits[6], (LANGS, D, R), jnp.float32) ** block_levels(splits[6], (LANGS, D, R), ((0, 8), (1, 16)), -0.2, 0.2)), 0.01, 1.0),
        "up_first": scatter_about(splits[7], (LANGS, R, KV), 0.5, 3.0, ((0, 8), (2, 16)), jnp.float32),
        "up_second": jnp.clip(jnp.exp(math.log(1.0) - 4.6051702 * jax.random.uniform(splits[8], (LANGS, R, KV), jnp.float32) ** block_levels(splits[8], (LANGS, R, KV), ((0, 8), (2, 16)), -0.2, 0.2)), 0.01, 1.0),
        "counts": uneven(splits[9], LANGS, (BLOCKS_DP * N_DP - LANGS) * BLK, (BLOCKS_DP * N_DP - LANGS) * BLK // 8, 2).astype(jnp.int32),
        "slot_language": jax.random.permutation(splits[10], LANGS).astype(jnp.int32),
    }


adapter_scale = 2.0
beta_first = 0.9
beta_second = 0.999
learn_rate = 0.001
adam_epsilon = 1e-08

def block_layout(counts, slot_language, first_block, block_total):
    block_count = ((counts + BLK - 1) // BLK).astype(jnp.int32)
    block_start = (jnp.cumsum(block_count) - block_count).astype(jnp.int32)
    block_index = (first_block + jnp.arange(block_total, dtype=jnp.int32)).astype(jnp.int32)
    language = (lax.optimization_barrier(jnp.sum((block_start[None, :] <= block_index[:, None]).astype(jnp.int32), axis=1)) - 1).astype(jnp.int32)
    lang_hot = language[:, None] == jnp.arange(counts.shape[0], dtype=jnp.int32)[None, :]
    lang_start = lax.optimization_barrier(jnp.sum(jnp.where(lang_hot, block_start[None, :], 0), axis=1)).astype(jnp.int32)
    lang_count = lax.optimization_barrier(jnp.sum(jnp.where(lang_hot, counts[None, :], 0), axis=1)).astype(jnp.int32)
    offset_rows = ((block_index - lang_start) * BLK).astype(jnp.int32)
    live_mask = offset_rows[:, None] + jnp.arange(BLK, dtype=jnp.int32)[None, :] < lang_count[:, None]
    slot_hot = slot_language[None, :] == language[:, None]
    slot_pick = lax.optimization_barrier(jnp.sum(jnp.where(slot_hot, jnp.arange(counts.shape[0], dtype=jnp.int32)[None, :], 0), axis=1)).astype(jnp.int32)
    return (live_mask, slot_pick, slot_hot)

def adam_update(param, first, second, gradient):
    new_first = beta_first * first + (1.0 - beta_first) * gradient
    new_second = beta_second * second + (1.0 - beta_second) * gradient * gradient
    first_hat = new_first / (1.0 - beta_first ** STEP)
    second_hat = new_second / (1.0 - beta_second ** STEP)
    new_param = param - learn_rate * first_hat / (jnp.sqrt(second_hat) + adam_epsilon)
    return (new_param, new_first, new_second)

def reference(activations, grad_out, base_weight, down_param, up_param, down_first, down_second, up_first, up_second, counts, slot_language):
    block_total = activations.shape[0] // BLK
    live_mask, slot_pick, slot_hot = block_layout(counts, slot_language, jnp.int32(0), block_total)
    down_low = down_param.astype(jnp.bfloat16)
    up_low = up_param.astype(jnp.bfloat16)
    contract_last = (((1,), (1,)), ((), ()))

    def advance(totals, scanned):
        down_gradient, up_gradient = totals
        activation_lines, grad_rows, live_rows, slot_one = scanned
        masked_values = jnp.where(live_rows[:, None], grad_rows, jnp.zeros((), jnp.bfloat16))
        down_one = lax.dynamic_index_in_dim(down_low, slot_one, 0, keepdims=False)
        up_one = lax.dynamic_index_in_dim(up_low, slot_one, 0, keepdims=False)
        reduced_rank_product = jnp.dot(activation_lines, down_one, preferred_element_type=jnp.float32).astype(jnp.bfloat16)
        backward_rank_product = lax.dot_general(masked_values, up_one, contract_last, preferred_element_type=jnp.float32).astype(jnp.bfloat16)
        frozen_contribution = lax.dot_general(masked_values, base_weight, contract_last, preferred_element_type=jnp.float32)
        adapter_contribution = lax.dot_general(backward_rank_product, down_one, contract_last, preferred_element_type=jnp.float32)
        key_output = (frozen_contribution + adapter_scale * adapter_contribution).astype(jnp.bfloat16)
        down_portion = adapter_scale * jnp.dot(activation_lines.T, backward_rank_product, preferred_element_type=jnp.float32)
        up_portion = adapter_scale * jnp.dot(reduced_rank_product.T, masked_values, preferred_element_type=jnp.float32)
        down_gradient = down_gradient.at[slot_one].add(down_portion)
        up_gradient = up_gradient.at[slot_one].add(up_portion)
        return ((down_gradient, up_gradient), key_output)
    initial = (jnp.zeros(down_param.shape, jnp.float32), jnp.zeros(up_param.shape, jnp.float32))
    scanned = (activations.reshape(block_total, BLK, D), grad_out.reshape(block_total, BLK, KV), live_mask, slot_pick)
    (down_gradient, up_gradient), outputs = lax.scan(advance, initial, scanned)
    input_gradient = outputs.reshape(block_total * BLK, D)
    new_down, new_down_first, new_down_second = adam_update(down_param, down_first, down_second, down_gradient)
    new_up, new_up_first, new_up_second = adam_update(up_param, up_first, up_second, up_gradient)
    return (input_gradient, new_down, new_up, new_down_first, new_down_second, new_up_first, new_up_second)
```

```python
import jax
import jax.numpy as jnp
from jax import lax
from jax.experimental import pallas as pl
from jax.experimental.pallas import tpu as pltpu
from jax.sharding import PartitionSpec as P

BLK = 128
STEP = 100
BLOCKS_DP = 64
LANGS = 16
RANK = 64
ROWS_OWN = 512
FEATURES = 512
KEYS = 1024

adapter_scale = 2.0
beta_first = 0.9
beta_second = 0.999
learn_rate = 0.001
adam_epsilon = 1e-08

MESH = pl.DeviceIdType.MESH
F32 = jnp.float32
BF16 = jnp.bfloat16
LAST = (((1,), (1,)), ((), ()))
FIRST = (((0,), (0,)), ((), ()))
CUT = 144
CHIPS = [(1, 0), (3, 0), (2, 0), (0, 1), (1, 1), (3, 1), (2, 1)]
PLANE = [(dy, dz) for dz in range(4) for dy in range(4) if (dy, dz) != (0, 0)]
DATA = [(dx, dl) for dl in range(2) for dx in range(4) if (dx, dl) != (0, 0)]


def adam_update(param, first, second, gradient):
    new_first = beta_first * first + (1.0 - beta_first) * gradient
    new_second = beta_second * second + (1.0 - beta_second) * gradient * gradient
    first_hat = new_first / (1.0 - beta_first**STEP)
    second_hat = new_second / (1.0 - beta_second**STEP)
    new_param = param - learn_rate * first_hat / (jnp.sqrt(second_hat) + adam_epsilon)
    return (new_param, new_first, new_second)


def block_layout(counts, slot_language, first_block):
    ids = jnp.arange(LANGS, dtype=jnp.int32)
    owner = slot_language[:, None]
    count = jnp.sum(jnp.where(ids[None, :] == owner, counts[None, :], 0), axis=1)
    start = jnp.sum(jnp.where(ids[None, :] < owner, (counts[None, :] + BLK - 1) // BLK, 0), axis=1)
    behind = first_block + jnp.arange(BLOCKS_DP, dtype=jnp.int32)[:, None] - start[None, :]
    left = count[None, :] - behind * BLK
    hot = (behind >= 0) & (left > 0)
    return (
        jnp.sum(jnp.where(hot, ids[None, :], 0), axis=1),
        jnp.sum(jnp.where(hot, left, 0), axis=1),
    )


def kernel(
    slot_ref, left_ref, acts_hbm, grad_hbm, base_hbm, down_hbm, up_hbm,
    out_hbm, down_out, up_out,
    G, ACT, BASE, WT, DOWN, UPOWN, UP, UMINE, USIB, DT, BK, LW, LOWN, LSIB, LGOT, LSUM, LARR,
    DG, DSEND, DARR, DZ, DZARR, UG, USEND, UARR, EXP, OB, send_sems, recv_sems, local_sems, out_sems,
):
    dp, f = lax.axis_index("dp"), lax.axis_index("fsdp")
    x, zl = lax.rem(dp, 4), dp // 4
    c, chip = lax.rem(f, 2), f // 2
    y, h = lax.rem(chip, 4), chip // 4
    z = h * 2 + zl

    def at(dx=0, dy=0, dz=0, dc=0):
        zz = lax.rem(z + dz, 4)
        return (
            lax.rem(zz, 2) * 4 + lax.rem(x + dx, 4),
            (zz // 2) * 8 + lax.rem(y + dy, 4) * 2 + lax.rem(c + dc, 2),
        )

    def flip(dx):
        return ((1 - zl) * 4 + lax.rem(x + dx, 4), f)

    def chip_of(dy, dh):
        return lax.rem(h + dh, 2) * 4 + lax.rem(y + dy, 4)

    makers = {}

    def message(name, src, dst, device):
        k = len(makers)
        makers[name] = lambda: pltpu.make_async_remote_copy(
            src_ref=src(),
            dst_ref=dst(),
            send_sem=send_sems.at[k],
            recv_sem=recv_sems.at[k],
            device_id=device(),
            device_id_type=MESH,
        )

    def same(name, ref, device):
        message(name, ref, ref, device)

    def start(*names):
        for name in names:
            makers[name]().start()

    def got(*names):
        for name in names:
            makers[name]().wait_recv()

    def rows(name, by, bh, lo, hi, **to):
        same(name, lambda: G.at[chip_of(by, bh) * 2 + c, pl.ds(lo, hi - lo)], lambda: at(**to))

    top, low_end, n = CUT, ROWS_OWN - CUT, ROWS_OWN
    half = n // 2
    plus, minus, across, sibling = dict(dy=1), dict(dy=3), dict(dz=2), dict(dc=1)
    rows("yp0", 0, 0, 0, half, **plus)
    rows("ym1", 0, 0, half, n, **minus)
    rows("zA0", 0, 0, 0, top, **across)
    rows("zA1", 0, 0, low_end, n, **across)
    rows("yp1", 0, 0, half, n, **plus)
    rows("ym0", 0, 0, 0, half, **minus)
    rows("zB", 0, 0, top, low_end, **across)
    rows("c0", 0, 0, 0, n, **sibling)
    rows("ap0", 0, 1, 0, top, **plus)
    rows("am0", 0, 1, 0, top, **minus)
    rows("ap1", 0, 1, low_end, n, **plus)
    rows("am1", 0, 1, low_end, n, **minus)
    rows("fp", 3, 0, 0, half, **plus)
    rows("fm", 1, 0, half, n, **minus)
    rows("zBm", 3, 0, top, low_end, **across)
    rows("zBp", 1, 0, top, low_end, **across)
    rows("c1", 3, 0, 0, n, **sibling)
    rows("c2", 1, 0, 0, n, **sibling)
    rows("c3", 0, 1, 0, n, **sibling)
    rows("fap", 3, 1, 0, top, **plus)
    rows("fam", 1, 1, low_end, n, **minus)
    rows("zB2", 2, 0, top, low_end, **across)
    rows("c4", 2, 0, 0, n, **sibling)
    rows("c5", 3, 1, 0, n, **sibling)
    rows("c6", 1, 1, 0, n, **sibling)
    rows("c7", 2, 1, 0, n, **sibling)
    message("u0", lambda: UMINE, lambda: USIB, lambda: at(dc=1))
    for k, (dy, dz) in enumerate(PLANE):
        same(
            f"u1_{k}",
            lambda: UP.at[dp, c, :, pl.ds(pl.multiple_of(chip * 128, 128), 128)],
            lambda dy=dy, dz=dz: at(dy=dy, dz=dz),
        )
    for dx in (1, 3, 2):
        for l in (0, 1):
            same(f"u2_{dx}_{l}", lambda l=l: UP.at[l * 4 + x, c], lambda dx=dx: at(dx=dx))
    same("u3", lambda: UP.at[:, c], lambda: at(dc=1))
    same("d0", lambda: DT.at[pl.ds(dp * 2, 2)], lambda: flip(0))
    for dx in (1, 3, 2):
        for l in (0, 1):
            same(
                f"d1_{dx}_{l}",
                lambda l=l: DT.at[pl.ds(((zl + l) % 2 * 4 + x) * 2, 2)],
                lambda dx=dx: at(dx=dx),
            )
    for k, (dy, dh) in enumerate(CHIPS):
        to = lambda dy=dy, dh=dh: at(dy=dy, dz=2 * dh)
        same(f"b_{k}", lambda: BK.at[chip, c], to)
        message(
            f"l1_{k}", lambda dy=dy, dh=dh: LSUM.at[chip_of(dy, dh)], lambda k=k: LARR.at[k], to
        )
        same(f"l2_{k}", lambda: LW.at[chip, c], to)
    same("b_c", lambda: BK.at[:, c], lambda: at(dc=1))
    same("l2_c", lambda: LW.at[:, c], lambda: at(dc=1))
    message("l0", lambda: LSIB, lambda: LGOT, lambda: at(dc=1))
    for k, dx in enumerate((1, 3, 2)):
        for l in (0, 1):
            message(
                f"r0_{k}_{l}",
                lambda dx=dx, l=l: DSEND.at[pl.ds((l * 4 + lax.rem(x + dx, 4)) * 2, 2)],
                lambda k=k, l=l: DARR.at[k, l],
                lambda dx=dx: at(dx=dx),
            )
    message("r1", lambda: DZ, lambda: DZARR, lambda: flip(0))
    for k, (dx, dl) in enumerate(DATA):
        message(
            f"v_{k}",
            lambda dx=dx, dl=dl: USEND.at[lax.rem(zl + dl, 2) * 4 + lax.rem(x + dx, 4)],
            lambda k=k: UARR.at[k],
            lambda dx=dx, dl=dl: (lax.rem(zl + dl, 2) * 4 + lax.rem(x + dx, 4), f),
        )

    loads = [
        pltpu.make_async_copy(up_hbm, UPOWN, local_sems.at[0]),
        pltpu.make_async_copy(grad_hbm, G.at[f], local_sems.at[1]),
        pltpu.make_async_copy(down_hbm, DOWN, local_sems.at[2]),
        pltpu.make_async_copy(base_hbm, BASE, local_sems.at[3]),
        pltpu.make_async_copy(acts_hbm, ACT, local_sems.at[4]),
    ]
    for load in loads:
        load.start()
    barrier = pltpu.get_barrier_semaphore()
    peers = [at(dy=dy, dz=dz) for dy, dz in PLANE] + [at(dc=1)]
    peers += [at(dx=dx) for dx in (1, 2, 3)] + [flip(dx) for dx in (1, 2, 3)]
    for peer in peers:
        pl.semaphore_signal(barrier, inc=1, device_id=peer, device_id_type=MESH)

    loads[0].wait()
    own_up = UPOWN[...].reshape(2 * RANK, RANK)
    none = jnp.zeros_like(own_up)
    first_core = jnp.where(c == 0, 1.0, 0.0).astype(F32)
    UMINE[...] = (
        jnp.concatenate([own_up, none], axis=1) * first_core
        + jnp.concatenate([none, own_up], axis=1) * (1.0 - first_core)
    ).astype(BF16)
    loads[1].wait()
    for j in range(4):
        inside = lax.broadcasted_iota(jnp.int32, (BLK, KEYS), 0) < left_ref[f * 4 + j]
        part = G[f, pl.ds(j * BLK, BLK)].astype(F32)
        G[f, pl.ds(j * BLK, BLK)] = jnp.where(inside, part, 0.0).astype(BF16)
    pl.semaphore_wait(barrier, len(peers))

    start("u0")
    loads[2].wait()
    for s in range(2):
        DT[dp * 2 + s] = DOWN[s].T.astype(BF16)
    start("d0")
    start("yp0", "ym1", "zA0", "zA1", "yp1", "ym0", "zB", "c0")
    got("u0")
    mine, theirs = UMINE[pl.ds(c * RANK, RANK)], USIB[pl.ds(c * RANK, RANK)]
    UP[dp, c, :, pl.ds(pl.multiple_of(chip * 128, 128), 128)] = (
        mine.astype(F32) + theirs.astype(F32)
    ).astype(BF16)
    start(*[f"u1_{k}" for k in range(len(PLANE))])
    got("d0")
    start(*[f"d1_{dx}_{l}" for dx in (1, 3, 2) for l in (0, 1)])
    got(*[f"u1_{k}" for k in range(len(PLANE))])
    start(*[f"u2_{dx}_{l}" for dx in (1, 3, 2) for l in (0, 1)])
    loads[3].wait()
    WT[...] = BASE[...].T
    got("zA0")
    start("ap0", "am0")
    got("zA1")
    start("ap1", "am1")
    got(*[f"d1_{dx}_{l}" for dx in (1, 3, 2) for l in (0, 1)])
    loads[4].wait()

    def partial_low(fb):
        parts = []
        for j in range(4):
            block = ACT[pl.ds(fb * ROWS_OWN + j * BLK, BLK)]
            parts.append(
                lax.dot_general(DT[slot_ref[fb * 4 + j]], block, LAST, preferred_element_type=F32)
            )
        return jnp.concatenate(parts, axis=1)

    def low_step(q, _):
        @pl.when(q == 2)
        def _():
            got("yp0")
            start("fp")
            got("ym1")
            start("fm")

        LSIB[q] = partial_low(q * 2 + 1 - c).astype(BF16)
        LOWN[q] = partial_low(q * 2 + c)
        return 0

    lax.fori_loop(0, 8, low_step, 0)
    start("l0")
    got("yp1")
    start("zBm", "c1")
    got("ym0")
    start("zBp", "c2")
    got("l0")

    def sum_step(q, _):
        total = LOWN[q] + LGOT[q].astype(F32)
        LOWN[q] = total
        LSUM[q] = total.astype(BF16)
        return 0

    lax.fori_loop(0, 8, sum_step, 0)
    start(*[f"l1_{k}" for k in range(7)])

    got(*[f"u2_{dx}_{l}" for dx in (1, 3, 2) for l in (0, 1)])
    start("u3")
    got("u3")
    for j in range(4):
        s = slot_ref[f * 4 + j]
        BK[chip, c, :, pl.ds(j * BLK, BLK)] = lax.dot_general(
            UP[s // 2, s % 2], G[f, pl.ds(j * BLK, BLK)], LAST, preferred_element_type=F32
        ).astype(BF16)
    start(*[f"b_{k}" for k in range(7)])
    got("zB")
    start("c3")
    got(*[f"l1_{k}" for k in range(7)])
    total = LOWN[chip]
    for k in range(7):
        total += LARR[k].astype(F32)
    LW[chip, c] = total.astype(BF16)
    start(*[f"l2_{k}" for k in range(7)])
    got(*[f"b_{k}" for k in range(7)])
    start("b_c")
    got("ap0")
    start("fap")
    got("am1")
    start("fam")
    got("b_c")

    def spread(source, fb):
        for j in range(4):
            slot = slot_ref[fb * 4 + j]
            part = source[fb // 2, fb % 2, :, pl.ds(j * BLK, BLK)].astype(F32)
            for s in range(LANGS):
                weight = jnp.where(slot == s, 1.0, 0.0).astype(F32)
                EXP[pl.ds(s * RANK, RANK), pl.ds(j * BLK, BLK)] = (part * weight).astype(BF16)

    def down_step(fb, _):
        @pl.when(fb == 6)
        def _():
            got("fp", "fm")
            start("zB2", "c4")

        @pl.when(fb == 10)
        def _():
            got(*[f"l2_{k}" for k in range(7)])
            start("l2_c")

        spread(BK, fb)
        part = jnp.dot(
            EXP[...], ACT[pl.ds(fb * ROWS_OWN, ROWS_OWN)], preferred_element_type=F32
        )

        @pl.when(fb == 0)
        def _():
            DG[...] = part

        @pl.when(fb > 0)
        def _():
            DG[...] += part

        return 0

    lax.fori_loop(0, 16, down_step, 0)

    def scale_step(s, _):
        total = adapter_scale * DG[pl.ds(s * RANK, RANK)]
        DG[pl.ds(s * RANK, RANK)] = total
        DSEND[s] = total.astype(BF16)
        return 0

    lax.fori_loop(0, LANGS, scale_step, 0)
    start(*[f"r0_{k}_{l}" for k in range(3) for l in (0, 1)])
    got("l2_c")

    order = [(0, 0), (3, 0), (1, 0), (0, 1), (2, 0), (3, 1), (1, 1), (2, 1)]

    def write(fb, slot):
        return pltpu.make_async_copy(
            OB.at[slot], out_hbm.at[pl.ds(fb * ROWS_OWN, ROWS_OWN)], out_sems.at[slot]
        )

    def down_sum(l):
        total = DG[pl.ds((l * 4 + x) * 2 * RANK, 2 * RANK)]
        for k in range(3):
            total += DARR[k, l].astype(F32).reshape(2 * RANK, FEATURES)
        return total

    def main_step(t, _):
        i, core = t // 2, t % 2
        dy = jnp.int32(0)
        dh = jnp.int32(0)
        for k, (a, b) in enumerate(order):
            dy = jnp.where(i == k, a, dy)
            dh = jnp.where(i == k, b, dh)
        fb = chip_of(dy, dh) * 2 + lax.rem(c + core, 2)

        @pl.when(t == 1)
        def _():
            got("c0")

        @pl.when(t == 3)
        def _():
            got("c1")

        @pl.when(t == 4)
        def _():
            got("ap1", "zBm")
            start("c5")

        @pl.when(t == 5)
        def _():
            got("c2", "am0", "zBp")
            start("c6")

        @pl.when(t == 7)
        def _():
            got("c3")
            got(*[f"r0_{k}_{l}" for k in range(3) for l in (0, 1)])
            DZ[...] = down_sum(1 - zl).astype(BF16)
            start("r1")

        @pl.when(t == 9)
        def _():
            got("c4")

        @pl.when(t == 11)
        def _():
            got("c5")

        @pl.when(t == 12)
        def _():
            got("fap", "fam", "zB2")
            start("c7")

        @pl.when(t == 13)
        def _():
            got("c6")

        @pl.when(t == 15)
        def _():
            got("c7")

        spread(LW, fb)
        part = jnp.dot(
            EXP[...],
            G[fb, :, pl.ds(pl.multiple_of(chip * 128, 128), 128)],
            preferred_element_type=F32,
        )

        @pl.when(t == 0)
        def _():
            UG[...] = part

        @pl.when(t > 0)
        def _():
            UG[...] += part

        @pl.when(t == 15)
        def _():
            lane = lax.broadcasted_iota(jnp.int32, (RANK, 128), 1)
            for d in range(8):
                even = adapter_scale * UG[pl.ds(d * 2 * RANK, RANK)]
                odd = adapter_scale * UG[pl.ds(d * 2 * RANK + RANK, RANK)]
                left = jnp.where(lane < RANK, even, pltpu.roll(odd, RANK, 1))
                right = jnp.where(lane < RANK, pltpu.roll(even, RANK, 1), odd)
                USEND[d] = left * first_core + right * (1.0 - first_core)
            start(*[f"v_{k}" for k in range(7)])

        slot = t % 2

        @pl.when(t >= 2)
        def _():
            write(fb, slot).wait()

        frozen = jnp.dot(G[fb], WT[...], preferred_element_type=F32)
        for j in range(4):
            low = lax.dot_general(
                BK[fb // 2, fb % 2, :, pl.ds(j * BLK, BLK)],
                DT[slot_ref[fb * 4 + j]],
                FIRST,
                preferred_element_type=F32,
            )
            OB[slot, pl.ds(j * BLK, BLK)] = (
                frozen[j * BLK : (j + 1) * BLK] + adapter_scale * low
            ).astype(BF16)
        write(fb, slot).start()
        return 0

    lax.fori_loop(0, 16, main_step, 0)
    got("r1")
    total = down_sum(zl) + DZARR[...].astype(F32)
    down_out[0] = total[:RANK].T
    down_out[1] = total[RANK:].T
    got(*[f"v_{k}" for k in range(7)])
    total = USEND[dp]
    for k in range(7):
        total += UARR[k]
    up_out[...] = total
    write(f, 0).wait()
    write(f, 1).wait()
    for name in makers:
        makers[name]().wait_send()


def on_device(
    activations,
    grad_out,
    base_weight,
    down_param,
    up_param,
    down_first,
    down_second,
    up_first,
    up_second,
    counts,
    slot_language,
):
    slots, left = block_layout(counts, slot_language, lax.axis_index("dp") * BLOCKS_DP)
    smem = pl.BlockSpec(memory_space=pltpu.SMEM)
    anywhere = pl.BlockSpec(memory_space=pl.ANY)
    vmem = pl.BlockSpec(memory_space=pltpu.VMEM)
    n_messages = 120
    input_gradient, down_own, up_own = pl.pallas_call(
        kernel,
        out_shape=(
            jax.ShapeDtypeStruct(activations.shape, BF16),
            jax.ShapeDtypeStruct((2, FEATURES, RANK), F32),
            jax.ShapeDtypeStruct((RANK, 128), F32),
        ),
        in_specs=[smem, smem] + [anywhere] * 5,
        out_specs=(anywhere, vmem, vmem),
        scratch_shapes=[
            pltpu.VMEM((16, ROWS_OWN, KEYS), BF16),
            pltpu.VMEM((16 * ROWS_OWN, FEATURES), BF16),
            pltpu.VMEM((FEATURES, KEYS), BF16),
            pltpu.VMEM((KEYS, FEATURES), BF16),
            pltpu.VMEM((2, FEATURES, RANK), F32),
            pltpu.VMEM((2, RANK, RANK), F32),
            pltpu.VMEM((8, 2, RANK, KEYS), BF16),
            pltpu.VMEM((2 * RANK, 128), BF16),
            pltpu.VMEM((2 * RANK, 128), BF16),
            pltpu.VMEM((LANGS, RANK, FEATURES), BF16),
            pltpu.VMEM((8, 2, RANK, ROWS_OWN), BF16),
            pltpu.VMEM((8, 2, RANK, ROWS_OWN), BF16),
            pltpu.VMEM((8, RANK, ROWS_OWN), F32),
            pltpu.VMEM((8, RANK, ROWS_OWN), BF16),
            pltpu.VMEM((8, RANK, ROWS_OWN), BF16),
            pltpu.VMEM((8, RANK, ROWS_OWN), BF16),
            pltpu.VMEM((7, RANK, ROWS_OWN), BF16),
            pltpu.VMEM((LANGS * RANK, FEATURES), F32),
            pltpu.VMEM((LANGS, RANK, FEATURES), BF16),
            pltpu.VMEM((3, 2, 2, RANK, FEATURES), BF16),
            pltpu.VMEM((2 * RANK, FEATURES), BF16),
            pltpu.VMEM((2 * RANK, FEATURES), BF16),
            pltpu.VMEM((LANGS * RANK, 128), F32),
            pltpu.VMEM((8, RANK, 128), F32),
            pltpu.VMEM((7, RANK, 128), F32),
            pltpu.VMEM((LANGS * RANK, ROWS_OWN), BF16),
            pltpu.VMEM((2, ROWS_OWN, FEATURES), BF16),
            pltpu.SemaphoreType.DMA((n_messages,)),
            pltpu.SemaphoreType.DMA((n_messages,)),
            pltpu.SemaphoreType.DMA((5,)),
            pltpu.SemaphoreType.DMA((2,)),
        ],
        compiler_params=pltpu.CompilerParams(
            collective_id=0, has_side_effects=True, vmem_limit_bytes=58 * 2**20
        ),
        cost_estimate=pl.CostEstimate(
            flops=2 * 8192 * 512 * 1024 * 3, bytes_accessed=40 * 2**20, transcendentals=0
        ),
    )(slots, left, activations, grad_out, base_weight, down_param, up_param)
    up_gradient = jnp.stack([up_own[:, :RANK], up_own[:, RANK:]])
    new_down, new_down_first, new_down_second = adam_update(
        down_param, down_first, down_second, down_own
    )
    new_up, new_up_first, new_up_second = adam_update(up_param, up_first, up_second, up_gradient)
    return (
        input_gradient,
        new_down,
        new_up,
        new_down_first,
        new_down_second,
        new_up_first,
        new_up_second,
    )


def solution(mesh):
    placed = (
        P("dp", "fsdp"),
        P(("dp", "fsdp"), None),
        P("fsdp", None),
        P("dp", "fsdp", None),
        P("dp", None, "fsdp"),
        P("dp", "fsdp", None),
        P("dp", "fsdp", None),
        P("dp", None, "fsdp"),
        P("dp", None, "fsdp"),
        P(),
        P(),
    )
    return jax.shard_map(
        on_device,
        mesh=mesh,
        in_specs=placed,
        out_specs=(
            P("dp", "fsdp"),
            P("dp", "fsdp", None),
            P("dp", None, "fsdp"),
            P("dp", "fsdp", None),
            P("dp", "fsdp", None),
            P("dp", None, "fsdp"),
            P("dp", None, "fsdp"),
        ),
        check_vma=False,
    )
```

```python
import jax
import jax.numpy as jnp
from jax import lax
from jax.experimental import pallas as pl
from jax.experimental.pallas import tpu as pltpu
from jax.sharding import PartitionSpec as P

BLK = 128
STEP = 100
BLOCKS_DP = 64
LANGS = 16
RANK = 64
ROWS_OWN = 512
GROUP = 4
FEATURES = 512
KEYS = 1024

adapter_scale = 2.0
beta_first = 0.9
beta_second = 0.999
learn_rate = 0.001
adam_epsilon = 1e-08

MESH = pl.DeviceIdType.MESH
F32 = jnp.float32
BF16 = jnp.bfloat16
LAST = (((1,), (1,)), ((), ()))
FIRST = (((0,), (0,)), ((), ()))
CUT = 144
RING = (1, 3, 2)
PLANE = [(dy, dz) for dz in range(4) for dy in range(4) if (dy, dz) != (0, 0)]
DATA = [(dx, dl) for dl in range(2) for dx in range(4) if (dx, dl) != (0, 0)]


def adam_update(param, first, second, gradient):
    new_first = beta_first * first + (1.0 - beta_first) * gradient
    new_second = beta_second * second + (1.0 - beta_second) * gradient * gradient
    first_hat = new_first / (1.0 - beta_first**STEP)
    second_hat = new_second / (1.0 - beta_second**STEP)
    new_param = param - learn_rate * first_hat / (jnp.sqrt(second_hat) + adam_epsilon)
    return (new_param, new_first, new_second)


def turn(a):
    return jnp.swapaxes(a, 1, 2)


def block_layout(counts, slot_language, first_block):
    ids = jnp.arange(LANGS, dtype=jnp.int32)
    owner = slot_language[:, None]
    count = jnp.sum(jnp.where(ids[None, :] == owner, counts[None, :], 0), axis=1)
    start = jnp.sum(jnp.where(ids[None, :] < owner, (counts[None, :] + BLK - 1) // BLK, 0), axis=1)
    behind = first_block + jnp.arange(BLOCKS_DP, dtype=jnp.int32)[:, None] - start[None, :]
    left = count[None, :] - behind * BLK
    hot = (behind >= 0) & (left > 0)
    return (
        jnp.sum(jnp.where(hot, ids[None, :], 0), axis=1),
        jnp.sum(jnp.where(hot, left, 0), axis=1),
    )


def kernel(
    slot_ref, left_ref, acts_hbm, grad_hbm, base_hbm, down_hbm, up_hbm,
    out_hbm, down_out, up_out,
    G, ACT, BASE, WT, DOWN, UPOWN, UP, UMINE, USIB, DT, BK, LW, LOWN, LSIB, LGOT, LSUM, LARR, LZ, LZARR,
    DG, DSEND, DARR, DZ, DZARR, UG, UOTHER, UHALF, USEND, UARR, EXP, OB, send_sems, recv_sems, local_sems, out_sems,
):
    dp, f = lax.axis_index("dp"), lax.axis_index("fsdp")
    x, zl = lax.rem(dp, 4), dp // 4
    c, chip = lax.rem(f, 2), f // 2
    y, h = lax.rem(chip, 4), chip // 4
    z = h * 2 + zl

    def at(dx=0, dy=0, dz=0, dc=0):
        zz = lax.rem(z + dz, 4)
        return (
            lax.rem(zz, 2) * 4 + lax.rem(x + dx, 4),
            (zz // 2) * 8 + lax.rem(y + dy, 4) * 2 + lax.rem(c + dc, 2),
        )

    def flip(dx):
        return ((1 - zl) * 4 + lax.rem(x + dx, 4), f)

    def chip_of(dy, dh):
        return lax.rem(h + dh, 2) * 4 + lax.rem(y + dy, 4)

    makers = {}

    def message(name, src, dst, device):
        k = len(makers)
        makers[name] = lambda: pltpu.make_async_remote_copy(
            src_ref=src(),
            dst_ref=dst(),
            send_sem=send_sems.at[k],
            recv_sem=recv_sems.at[k],
            device_id=device(),
            device_id_type=MESH,
        )

    def same(name, ref, device):
        message(name, ref, ref, device)

    def start(*names):
        for name in names:
            makers[name]().start()

    def got(*names):
        for name in names:
            makers[name]().wait_recv()

    def rows(name, by, bh, lo, hi, **to):
        same(name, lambda: G.at[chip_of(by, bh) * 2 + c, pl.ds(lo, hi - lo)], lambda: at(**to))

    top, low_end, n = CUT, ROWS_OWN - CUT, ROWS_OWN
    half = n // 2
    plus, minus, across, sibling = dict(dy=1), dict(dy=3), dict(dz=2), dict(dc=1)
    rows("yp0", 0, 0, 0, half, **plus)
    rows("ym1", 0, 0, half, n, **minus)
    rows("zA0", 0, 0, 0, top, **across)
    rows("zA1", 0, 0, low_end, n, **across)
    rows("yp1", 0, 0, half, n, **plus)
    rows("ym0", 0, 0, 0, half, **minus)
    rows("zB", 0, 0, top, low_end, **across)
    rows("c0", 0, 0, 0, n, **sibling)
    rows("ap0", 0, 1, 0, top, **plus)
    rows("am0", 0, 1, 0, top, **minus)
    rows("ap1", 0, 1, low_end, n, **plus)
    rows("am1", 0, 1, low_end, n, **minus)
    rows("fp", 3, 0, 0, half, **plus)
    rows("fm", 1, 0, half, n, **minus)
    rows("zBm", 3, 0, top, low_end, **across)
    rows("zBp", 1, 0, top, low_end, **across)
    rows("c1", 3, 0, 0, n, **sibling)
    rows("c2", 1, 0, 0, n, **sibling)
    rows("c3", 0, 1, 0, n, **sibling)
    rows("fap", 3, 1, 0, top, **plus)
    rows("fam", 1, 1, low_end, n, **minus)
    rows("zB2", 2, 0, top, low_end, **across)
    rows("c4", 2, 0, 0, n, **sibling)
    rows("c5", 3, 1, 0, n, **sibling)
    rows("c6", 1, 1, 0, n, **sibling)
    rows("c7m", 2, 1, top, low_end, **sibling)
    rows("c70", 2, 1, 0, top, **sibling)
    rows("c71", 2, 1, low_end, n, **sibling)
    message("u0", lambda: UMINE, lambda: USIB, lambda: at(dc=1))
    for k, (dy, dz) in enumerate(PLANE):
        same(
            f"u1_{k}",
            lambda: UP.at[dp, c, :, pl.ds(pl.multiple_of(chip * 128, 128), 128)],
            lambda dy=dy, dz=dz: at(dy=dy, dz=dz),
        )
    for dx in (1, 3, 2):
        for l in (0, 1):
            same(f"u2_{dx}_{l}", lambda l=l: UP.at[l * 4 + x, c], lambda dx=dx: at(dx=dx))
    same("u3", lambda: UP.at[:, c], lambda: at(dc=1))
    same("d0", lambda: DT.at[pl.ds(dp * 2, 2)], lambda: flip(0))
    for dx in (1, 3, 2):
        for l in (0, 1):
            same(
                f"d1_{dx}_{l}",
                lambda l=l: DT.at[pl.ds(((zl + l) % 2 * 4 + x) * 2, 2)],
                lambda dx=dx: at(dx=dx),
            )
    other = chip_of(0, 1)
    for k, dy in enumerate(RING):
        to = lambda dy=dy: at(dy=dy)
        for l in (0, 1):
            message(
                f"ly_{k}_{l}",
                lambda dy=dy, l=l: LSUM.at[chip_of(dy, l)],
                lambda k=k, l=l: LARR.at[k, l],
                to,
            )
            same(f"b_{k}_{l}", lambda l=l: BK.at[chip_of(0, l), c], to)
            same(f"w_{k}_{l}", lambda l=l: LW.at[chip_of(0, l)], to)
    message("lz", lambda: LZ, lambda: LZARR, lambda: at(dz=2))
    same("bz", lambda: BK.at[chip, c], lambda: at(dz=2))
    same("wz", lambda: LW.at[chip], lambda: at(dz=2))
    message("ux", lambda: UOTHER, lambda: UHALF, lambda: at(dc=1))
    same("b_c", lambda: BK.at[:, c], lambda: at(dc=1))
    message("l0", lambda: LSIB, lambda: LGOT, lambda: at(dc=1))
    for k, dx in enumerate((1, 3, 2)):
        for l in (0, 1):
            message(
                f"r0_{k}_{l}",
                lambda dx=dx, l=l: DSEND.at[pl.ds((l * 4 + lax.rem(x + dx, 4)) * 2, 2)],
                lambda k=k, l=l: DARR.at[k, l],
                lambda dx=dx: at(dx=dx),
            )
    message("r1", lambda: DZ, lambda: DZARR, lambda: flip(0))
    for k, (dx, dl) in enumerate(DATA):
        message(
            f"v_{k}",
            lambda dx=dx, dl=dl: USEND.at[lax.rem(zl + dl, 2) * 4 + lax.rem(x + dx, 4)],
            lambda k=k: UARR.at[k],
            lambda dx=dx, dl=dl: (lax.rem(zl + dl, 2) * 4 + lax.rem(x + dx, 4), f),
        )

    loads = [
        pltpu.make_async_copy(up_hbm, UPOWN, local_sems.at[0]),
        pltpu.make_async_copy(grad_hbm, G.at[f], local_sems.at[1]),
        pltpu.make_async_copy(down_hbm, DOWN, local_sems.at[2]),
        pltpu.make_async_copy(base_hbm, BASE, local_sems.at[3]),
        pltpu.make_async_copy(acts_hbm, ACT, local_sems.at[4]),
    ]
    for load in loads:
        load.start()
    barrier = pltpu.get_barrier_semaphore()
    peers = [at(dy=dy, dz=dz) for dy, dz in PLANE] + [at(dc=1)]
    peers += [at(dx=dx) for dx in (1, 2, 3)] + [flip(dx) for dx in (1, 2, 3)]
    for peer in peers:
        pl.semaphore_signal(barrier, inc=1, device_id=peer, device_id_type=MESH)

    loads[0].wait()
    own_up = UPOWN[...].reshape(2 * RANK, RANK)
    none = jnp.zeros_like(own_up)
    first_core = jnp.where(c == 0, 1.0, 0.0).astype(F32)
    UMINE[...] = (
        jnp.concatenate([own_up, none], axis=1) * first_core
        + jnp.concatenate([none, own_up], axis=1) * (1.0 - first_core)
    ).astype(BF16)
    loads[2].wait()
    for s in range(2):
        DT[dp * 2 + s] = DOWN[s].astype(BF16)
    pl.semaphore_wait(barrier, len(peers))
    start("u0", "d0")
    loads[1].wait()
    for j in range(4):
        inside = lax.broadcasted_iota(jnp.int32, (BLK, KEYS), 0) < left_ref[f * 4 + j]
        part = G[f, pl.ds(j * BLK, BLK)].astype(F32)
        G[f, pl.ds(j * BLK, BLK)] = jnp.where(inside, part, 0.0).astype(BF16)
    got("u0")
    mine, theirs = UMINE[pl.ds(c * RANK, RANK)], USIB[pl.ds(c * RANK, RANK)]
    UP[dp, c, :, pl.ds(pl.multiple_of(chip * 128, 128), 128)] = (
        mine.astype(F32) + theirs.astype(F32)
    ).astype(BF16)
    start(*[f"u1_{k}" for k in range(len(PLANE))])
    start("yp0", "ym1", "zA0", "zA1")
    got("d0")
    start(*[f"d1_{dx}_{l}" for dx in (1, 3, 2) for l in (0, 1)])
    start("yp1", "ym0", "zB", "c0")
    loads[3].wait()
    WT[...] = BASE[...].T
    got(*[f"u1_{k}" for k in range(len(PLANE))])
    start(*[f"u2_{dx}_{l}" for dx in (1, 3, 2) for l in (0, 1)])
    got(*[f"d1_{dx}_{l}" for dx in (1, 3, 2) for l in (0, 1)])
    loads[4].wait()

    def partial_low(fb):
        parts = []
        for j in range(4):
            block = ACT[pl.ds(fb * ROWS_OWN + j * BLK, BLK)]
            parts.append(
                lax.dot_general(DT[slot_ref[fb * 4 + j]], block, LAST, preferred_element_type=F32)
            )
        return jnp.concatenate(parts, axis=1)

    def low_step(q, _):
        LSIB[q] = partial_low(q * 2 + 1 - c).astype(BF16)
        LOWN[q] = partial_low(q * 2 + c)
        return 0

    lax.fori_loop(0, 8, low_step, 0)
    start("l0")
    got("zA0", "yp0", "ym1")
    got("l0")

    def sum_step(q, _):
        total = LOWN[q] + LGOT[q].astype(F32)
        LOWN[q] = total
        LSUM[q] = total.astype(BF16)
        return 0

    lax.fori_loop(0, 8, sum_step, 0)
    both = [f"{k}_{l}" for k in range(3) for l in (0, 1)]
    start(*["ly_" + k for k in both])

    got(*[f"u2_{dx}_{l}" for dx in (1, 3, 2) for l in (0, 1)])
    start("u3")
    got("zA1", "u3")
    for j in range(4):
        s = slot_ref[f * 4 + j]
        BK[chip, c, :, pl.ds(j * BLK, BLK)] = lax.dot_general(
            UP[s // 2, s % 2], G[f, pl.ds(j * BLK, BLK)], LAST, preferred_element_type=F32
        ).astype(BF16)
    start("bz", *[f"b_{k}_0" for k in range(3)])
    got("yp1")
    start("c1")
    got("ym0")
    start("c2")
    got("bz")
    start(*[f"b_{k}_1" for k in range(3)])
    start("fp", "fm")
    got(*["ly_" + k for k in both])
    total = LOWN[other]
    for k in range(3):
        total += LARR[k, 1].astype(F32)
    LZ[...] = total.astype(BF16)
    start("lz", "zBm")
    got("zB")
    start("c3")
    total = LOWN[chip]
    for k in range(3):
        total += LARR[k, 0].astype(F32)
    got("lz")
    LW[chip] = (total + LZARR[...].astype(F32)).astype(BF16)
    start("wz", *[f"w_{k}_0" for k in range(3)])
    start("zBp")
    got(*["b_" + k for k in both])
    start("b_c", "ap0", "am1")
    got("b_c")

    def spread(read, fb, at_column):
        for j in range(4):
            slot = slot_ref[fb * 4 + j]
            part = read(pl.ds(j * BLK, BLK)).astype(F32)
            for s in range(LANGS):
                weight = jnp.where(slot == s, 1.0, 0.0).astype(F32)
                EXP[pl.ds(s * RANK, RANK), pl.ds(at_column + j * BLK, BLK)] = (
                    part * weight
                ).astype(BF16)

    span = GROUP * ROWS_OWN

    def down_step(g, _):
        @pl.when(g == 16 // GROUP - 1)
        def _():
            got("wz")
            start(*[f"w_{k}_1" for k in range(3)])
            start("ap1", "am0")

        for i in range(GROUP):
            fb = g * GROUP + i
            spread(lambda cols: BK[fb // 2, fb % 2, :, cols], fb, i * ROWS_OWN)
        part = jnp.dot(EXP[...], ACT[pl.ds(g * span, span)], preferred_element_type=F32)

        @pl.when(g == 0)
        def _():
            DG[...] = part

        @pl.when(g > 0)
        def _():
            DG[...] += part

        return 0

    lax.fori_loop(0, 16 // GROUP, down_step, 0)

    def scale_step(s, _):
        total = adapter_scale * DG[pl.ds(s * RANK, RANK)]
        DG[pl.ds(s * RANK, RANK)] = total
        DSEND[s] = total.astype(BF16)
        return 0

    lax.fori_loop(0, LANGS, scale_step, 0)
    start(*[f"r0_{k}_{l}" for k in range(3) for l in (0, 1)])
    got(*[f"w_{k}_0" for k in range(3)])
    got("fp", "fm")
    start("zB2", "c4")

    order = [(0, 0), (3, 0), (1, 0), (0, 1), (2, 0), (3, 1), (1, 1), (2, 1)]

    def write(fb, slot):
        return pltpu.make_async_copy(
            OB.at[slot], out_hbm.at[pl.ds(fb * ROWS_OWN, ROWS_OWN)], out_sems.at[slot]
        )

    def down_sum(l):
        total = DG[pl.ds((l * 4 + x) * 2 * RANK, 2 * RANK)]
        for k in range(3):
            total += DARR[k, l].astype(F32).reshape(2 * RANK, FEATURES)
        return total

    def main_step(t, _):
        i, core = t // 2, t % 2
        dy = jnp.int32(0)
        dh = jnp.int32(0)
        for k, (a, b) in enumerate(order):
            dy = jnp.where(i == k, a, dy)
            dh = jnp.where(i == k, b, dh)
        fb = chip_of(dy, dh) * 2 + lax.rem(c + core, 2)

        @pl.when(t == 1)
        def _():
            got("c0")

        @pl.when(t == 2)
        def _():
            got("ap0")
            start("fap")
            got("am1")
            start("fam")

        @pl.when(t == 3)
        def _():
            got("c1")

        @pl.when(t == 5)
        def _():
            got("c2")

        @pl.when(t == 6)
        def _():
            got(*[f"w_{k}_1" for k in range(3)])

        @pl.when(t == 7)
        def _():
            got("c3")

        @pl.when(t == 9)
        def _():
            got("c4")
            got(*[f"r0_{k}_{l}" for k in range(3) for l in (0, 1)])
            DZ[...] = down_sum(1 - zl).astype(BF16)
            start("r1")

        @pl.when(t == 10)
        def _():
            got("zBm", "ap1")
            start("c5")

        @pl.when(t == 11)
        def _():
            got("c5")

        @pl.when(t == 12)
        def _():
            got("zBp", "am0")
            start("c6")

        @pl.when(t == 13)
        def _():
            got("c6")

        @pl.when(t == 14)
        def _():
            got("r1")
            total = down_sum(zl) + DZARR[...].astype(F32)
            down_out[0] = total[:RANK]
            down_out[1] = total[RANK:]
            got("zB2")
            start("c7m")
            got("fap")
            start("c70")
            got("fam")
            start("c71")

        @pl.when(t == 15)
        def _():
            got("ux")
            USEND[...] += UHALF[...]
            start(*[f"v_{k}" for k in range(7)])
            got("c7m", "c70", "c71")

        @pl.when(core == 0)
        def _():
            spread(lambda cols: LW[fb // 2, :, cols], fb, 0)
            part = jnp.dot(
                EXP[:, :ROWS_OWN],
                G[fb, :, pl.ds(pl.multiple_of(chip * 128, 128), 128)],
                preferred_element_type=F32,
            )

            @pl.when(t == 0)
            def _():
                UG[...] = part

            @pl.when(t > 0)
            def _():
                UG[...] += part

        @pl.when(t == 14)
        def _():
            lane = lax.broadcasted_iota(jnp.int32, (RANK, 128), 1)
            for d in range(8):
                even = adapter_scale * UG[pl.ds(d * 2 * RANK, RANK)]
                odd = adapter_scale * UG[pl.ds(d * 2 * RANK + RANK, RANK)]
                left = jnp.where(lane < RANK, even, pltpu.roll(odd, RANK, 1))
                right = jnp.where(lane < RANK, pltpu.roll(even, RANK, 1), odd)
                USEND[d] = left * first_core + right * (1.0 - first_core)
                UOTHER[d] = right * first_core + left * (1.0 - first_core)
            start("ux")

        slot = t % 2

        @pl.when(t >= 2)
        def _():
            write(fb, slot).wait()

        frozen = jnp.dot(G[fb], WT[...], preferred_element_type=F32)
        for j in range(4):
            low = lax.dot_general(
                BK[fb // 2, fb % 2, :, pl.ds(j * BLK, BLK)],
                DT[slot_ref[fb * 4 + j]],
                FIRST,
                preferred_element_type=F32,
            )
            OB[slot, pl.ds(j * BLK, BLK)] = (
                frozen[j * BLK : (j + 1) * BLK] + adapter_scale * low
            ).astype(BF16)
        write(fb, slot).start()
        return 0

    lax.fori_loop(0, 16, main_step, 0)
    got(*[f"v_{k}" for k in range(7)])
    total = USEND[dp]
    for k in range(7):
        total += UARR[k]
    up_out[...] = total
    write(f, 0).wait()
    write(f, 1).wait()
    for name in makers:
        makers[name]().wait_send()


def on_device(
    activations,
    grad_out,
    base_weight,
    down_param,
    up_param,
    down_first,
    down_second,
    up_first,
    up_second,
    counts,
    slot_language,
):
    slots, left = block_layout(counts, slot_language, lax.axis_index("dp") * BLOCKS_DP)
    smem = pl.BlockSpec(memory_space=pltpu.SMEM)
    anywhere = pl.BlockSpec(memory_space=pl.ANY)
    vmem = pl.BlockSpec(memory_space=pltpu.VMEM)
    n_messages = 120
    input_gradient, down_own, up_own = pl.pallas_call(
        kernel,
        out_shape=(
            jax.ShapeDtypeStruct(activations.shape, BF16),
            jax.ShapeDtypeStruct((2, RANK, FEATURES), F32),
            jax.ShapeDtypeStruct((RANK, 128), F32),
        ),
        in_specs=[smem, smem] + [anywhere] * 5,
        out_specs=(anywhere, vmem, vmem),
        scratch_shapes=[
            pltpu.VMEM((16, ROWS_OWN, KEYS), BF16),
            pltpu.VMEM((16 * ROWS_OWN, FEATURES), BF16),
            pltpu.VMEM((FEATURES, KEYS), BF16),
            pltpu.VMEM((KEYS, FEATURES), BF16),
            pltpu.VMEM((2, RANK, FEATURES), F32),
            pltpu.VMEM((2, RANK, RANK), F32),
            pltpu.VMEM((8, 2, RANK, KEYS), BF16),
            pltpu.VMEM((2 * RANK, 128), BF16),
            pltpu.VMEM((2 * RANK, 128), BF16),
            pltpu.VMEM((LANGS, RANK, FEATURES), BF16),
            pltpu.VMEM((8, 2, RANK, ROWS_OWN), BF16),
            pltpu.VMEM((8, RANK, ROWS_OWN), BF16),
            pltpu.VMEM((8, RANK, ROWS_OWN), F32),
            pltpu.VMEM((8, RANK, ROWS_OWN), BF16),
            pltpu.VMEM((8, RANK, ROWS_OWN), BF16),
            pltpu.VMEM((8, RANK, ROWS_OWN), BF16),
            pltpu.VMEM((3, 2, RANK, ROWS_OWN), BF16),
            pltpu.VMEM((RANK, ROWS_OWN), BF16),
            pltpu.VMEM((RANK, ROWS_OWN), BF16),
            pltpu.VMEM((LANGS * RANK, FEATURES), F32),
            pltpu.VMEM((LANGS, RANK, FEATURES), BF16),
            pltpu.VMEM((3, 2, 2, RANK, FEATURES), BF16),
            pltpu.VMEM((2 * RANK, FEATURES), BF16),
            pltpu.VMEM((2 * RANK, FEATURES), BF16),
            pltpu.VMEM((LANGS * RANK, 128), F32),
            pltpu.VMEM((8, RANK, 128), F32),
            pltpu.VMEM((8, RANK, 128), F32),
            pltpu.VMEM((8, RANK, 128), F32),
            pltpu.VMEM((7, RANK, 128), F32),
            pltpu.VMEM((LANGS * RANK, GROUP * ROWS_OWN), BF16),
            pltpu.VMEM((2, ROWS_OWN, FEATURES), BF16),
            pltpu.SemaphoreType.DMA((n_messages,)),
            pltpu.SemaphoreType.DMA((n_messages,)),
            pltpu.SemaphoreType.DMA((5,)),
            pltpu.SemaphoreType.DMA((2,)),
        ],
        compiler_params=pltpu.CompilerParams(
            collective_id=0, has_side_effects=True, vmem_limit_bytes=58 * 2**20
        ),
        cost_estimate=pl.CostEstimate(
            flops=2 * 8192 * 512 * 1024 * 3, bytes_accessed=40 * 2**20, transcendentals=0
        ),
    )(slots, left, activations, grad_out, base_weight, turn(down_param), up_param)
    up_gradient = jnp.stack([up_own[:, :RANK], up_own[:, RANK:]])
    new_down, new_down_first, new_down_second = map(
        turn, adam_update(turn(down_param), turn(down_first), turn(down_second), down_own)
    )
    new_up, new_up_first, new_up_second = adam_update(up_param, up_first, up_second, up_gradient)
    return (
        input_gradient,
        new_down,
        new_up,
        new_down_first,
        new_down_second,
        new_up_first,
        new_up_second,
    )


def solution(mesh):
    placed = (
        P("dp", "fsdp"),
        P(("dp", "fsdp"), None),
        P("fsdp", None),
        P("dp", "fsdp", None),
        P("dp", None, "fsdp"),
        P("dp", "fsdp", None),
        P("dp", "fsdp", None),
        P("dp", None, "fsdp"),
        P("dp", None, "fsdp"),
        P(),
        P(),
    )
    return jax.shard_map(
        on_device,
        mesh=mesh,
        in_specs=placed,
        out_specs=(
            P("dp", "fsdp"),
            P("dp", "fsdp", None),
            P("dp", None, "fsdp"),
            P("dp", "fsdp", None),
            P("dp", "fsdp", None),
            P("dp", None, "fsdp"),
            P("dp", None, "fsdp"),
        ),
        check_vma=False,
    )
```

```python
import jax
import jax.numpy as jnp
from jax import lax
from jax.experimental import pallas as pl
from jax.experimental.pallas import tpu as pltpu
from jax.sharding import PartitionSpec as P

BLK = 128
STEP = 100
BLOCKS_DP = 64
LANGS = 16
RANK = 64
ROWS_OWN = 512
GROUP = 4
FEATURES = 512
KEYS = 1024

adapter_scale = 2.0
beta_first = 0.9
beta_second = 0.999
learn_rate = 0.001
adam_epsilon = 1e-08

MESH = pl.DeviceIdType.MESH
F32 = jnp.float32
BF16 = jnp.bfloat16
LAST = (((1,), (1,)), ((), ()))
FIRST = (((0,), (0,)), ((), ()))
CUT = 144
RING = (1, 3, 2)
DATA = [(dx, dl) for dl in range(2) for dx in range(4) if (dx, dl) != (0, 0)]


def adam_update(param, first, second, gradient):
    new_first = beta_first * first + (1.0 - beta_first) * gradient
    new_second = beta_second * second + (1.0 - beta_second) * gradient * gradient
    first_hat = new_first / (1.0 - beta_first**STEP)
    second_hat = new_second / (1.0 - beta_second**STEP)
    new_param = param - learn_rate * first_hat / (jnp.sqrt(second_hat) + adam_epsilon)
    return (new_param, new_first, new_second)


def turn(a):
    return jnp.swapaxes(a, 1, 2)


def block_layout(counts, slot_language, first_block):
    ids = jnp.arange(LANGS, dtype=jnp.int32)
    owner = slot_language[:, None]
    count = jnp.sum(jnp.where(ids[None, :] == owner, counts[None, :], 0), axis=1)
    start = jnp.sum(jnp.where(ids[None, :] < owner, (counts[None, :] + BLK - 1) // BLK, 0), axis=1)
    behind = first_block + jnp.arange(BLOCKS_DP, dtype=jnp.int32)[:, None] - start[None, :]
    left = count[None, :] - behind * BLK
    hot = (behind >= 0) & (left > 0)
    return (
        jnp.sum(jnp.where(hot, ids[None, :], 0), axis=1),
        jnp.sum(jnp.where(hot, left, 0), axis=1),
    )


def kernel(
    slot_ref, left_ref, acts_hbm, grad_hbm, base_hbm, down_hbm, up_hbm,
    out_hbm, down_out, up_out,
    G, ACT, BASE, WT, DOWN, UPOWN, UP, UMINE, USIB, DT, BK, LW, LOWN, LSIB, LGOT, LSUM, LARR, LZ, LZARR,
    DG, DSEND, DARR, DZ, DZARR, UG, FAR, COLUMNS, UOTHER, UHALF, USEND, UARR, EXP, OB, send_sems, recv_sems, local_sems, out_sems,
):
    dp, f = lax.axis_index("dp"), lax.axis_index("fsdp")
    x, zl = lax.rem(dp, 4), dp // 4
    c, chip = lax.rem(f, 2), f // 2
    y, h = lax.rem(chip, 4), chip // 4
    z = h * 2 + zl

    def at(dx=0, dy=0, dz=0, dc=0):
        zz = lax.rem(z + dz, 4)
        return (
            lax.rem(zz, 2) * 4 + lax.rem(x + dx, 4),
            (zz // 2) * 8 + lax.rem(y + dy, 4) * 2 + lax.rem(c + dc, 2),
        )

    def flip(dx):
        return ((1 - zl) * 4 + lax.rem(x + dx, 4), f)

    def chip_of(dy, dh):
        return lax.rem(h + dh, 2) * 4 + lax.rem(y + dy, 4)

    makers = {}

    def message(name, src, dst, device):
        k = len(makers)
        makers[name] = lambda: pltpu.make_async_remote_copy(
            src_ref=src(),
            dst_ref=dst(),
            send_sem=send_sems.at[k],
            recv_sem=recv_sems.at[k],
            device_id=device(),
            device_id_type=MESH,
        )

    def same(name, ref, device):
        message(name, ref, ref, device)

    def start(*names):
        for name in names:
            makers[name]().start()

    def got(*names):
        for name in names:
            makers[name]().wait_recv()

    def rows(name, by, bh, lo, hi, **to):
        same(name, lambda: G.at[chip_of(by, bh) * 2 + c, pl.ds(lo, hi - lo)], lambda: at(**to))

    top, low_end, n = CUT, ROWS_OWN - CUT, ROWS_OWN
    half = n // 2
    plus, minus, across, sibling = dict(dy=1), dict(dy=3), dict(dz=2), dict(dc=1)
    rows("yp0", 0, 0, 0, half, **plus)
    rows("ym1", 0, 0, half, n, **minus)
    rows("zA0", 0, 0, 0, top, **across)
    rows("zA1", 0, 0, low_end, n, **across)
    rows("yp1", 0, 0, half, n, **plus)
    rows("ym0", 0, 0, 0, half, **minus)
    rows("zB", 0, 0, top, low_end, **across)
    rows("c0", 0, 0, 0, n, **sibling)
    rows("ap0", 0, 1, 0, top, **plus)
    rows("am0", 0, 1, 0, top, **minus)
    rows("ap1", 0, 1, low_end, n, **plus)
    rows("am1", 0, 1, low_end, n, **minus)
    rows("fp", 3, 0, 0, half, **plus)
    rows("fm", 1, 0, half, n, **minus)
    rows("zBm", 3, 0, top, low_end, **across)
    rows("zBp", 1, 0, top, low_end, **across)
    rows("c1", 3, 0, 0, n, **sibling)
    rows("c2", 1, 0, 0, n, **sibling)
    rows("c3", 0, 1, 0, n, **sibling)
    rows("fap", 3, 1, 0, top, **plus)
    rows("fam", 1, 1, low_end, n, **minus)
    rows("zB2", 2, 0, top, low_end, **across)
    rows("c4", 2, 0, 0, n, **sibling)
    rows("c5", 3, 1, 0, n, **sibling)
    rows("c6", 1, 1, 0, n, **sibling)
    rows("c7m", 2, 1, top, low_end, **sibling)
    rows("c70", 2, 1, 0, top, **sibling)
    rows("c71", 2, 1, low_end, n, **sibling)
    message("u0", lambda: UMINE, lambda: USIB, lambda: at(dc=1))
    for k, dy in enumerate(RING):
        same(
            f"uy_{k}",
            lambda: UP.at[dp, c, :, pl.ds(pl.multiple_of(chip * 128, 128), 128)],
            lambda dy=dy: at(dy=dy),
        )
    for k, dz in enumerate((1, 3, 2)):
        same(
            f"uz_{k}",
            lambda: UP.at[dp, c, :, pl.ds(pl.multiple_of(h * 512, 128), 512)],
            lambda dz=dz: at(dz=dz),
        )
    message(
        "q",
        lambda: G.at[f, :, pl.ds(pl.multiple_of(chip_of(2, 1) * 128, 128), 128)],
        lambda: FAR,
        lambda: at(dy=2, dz=2),
    )
    for dx in (1, 3, 2):
        for l in (0, 1):
            same(f"u2_{dx}_{l}", lambda l=l: UP.at[l * 4 + x, c], lambda dx=dx: at(dx=dx))
    same("u3", lambda: UP.at[:, c], lambda: at(dc=1))
    same("d0", lambda: DT.at[pl.ds(dp * 2, 2)], lambda: flip(0))
    for dx in (1, 3, 2):
        for l in (0, 1):
            same(
                f"d1_{dx}_{l}",
                lambda l=l: DT.at[pl.ds(((zl + l) % 2 * 4 + x) * 2, 2)],
                lambda dx=dx: at(dx=dx),
            )
    other = chip_of(0, 1)
    for k, dy in enumerate(RING):
        to = lambda dy=dy: at(dy=dy)
        for l in (0, 1):
            message(
                f"ly_{k}_{l}",
                lambda dy=dy, l=l: LSUM.at[chip_of(dy, l)],
                lambda k=k, l=l: LARR.at[k, l],
                to,
            )
            same(f"b_{k}_{l}", lambda l=l: BK.at[chip_of(0, l), c], to)
            same(f"w_{k}_{l}", lambda l=l: LW.at[chip_of(0, l)], to)
    message("lz", lambda: LZ, lambda: LZARR, lambda: at(dz=2))
    same("bz", lambda: BK.at[chip, c], lambda: at(dz=2))
    same("wz", lambda: LW.at[chip], lambda: at(dz=2))
    message("ux", lambda: UOTHER, lambda: UHALF, lambda: at(dc=1))
    same("b_c", lambda: BK.at[:, c], lambda: at(dc=1))
    message("l0", lambda: LSIB, lambda: LGOT, lambda: at(dc=1))
    for k, dx in enumerate((1, 3, 2)):
        for l in (0, 1):
            message(
                f"r0_{k}_{l}",
                lambda dx=dx, l=l: DSEND.at[pl.ds((l * 4 + lax.rem(x + dx, 4)) * 2, 2)],
                lambda k=k, l=l: DARR.at[k, l],
                lambda dx=dx: at(dx=dx),
            )
    message("r1", lambda: DZ, lambda: DZARR, lambda: flip(0))
    for k, (dx, dl) in enumerate(DATA):
        message(
            f"v_{k}",
            lambda dx=dx, dl=dl: USEND.at[lax.rem(zl + dl, 2) * 4 + lax.rem(x + dx, 4)],
            lambda k=k: UARR.at[k],
            lambda dx=dx, dl=dl: (lax.rem(zl + dl, 2) * 4 + lax.rem(x + dx, 4), f),
        )

    loads = [
        pltpu.make_async_copy(up_hbm, UPOWN, local_sems.at[0]),
        pltpu.make_async_copy(grad_hbm, G.at[f], local_sems.at[1]),
        pltpu.make_async_copy(down_hbm, DOWN, local_sems.at[2]),
        pltpu.make_async_copy(base_hbm, BASE, local_sems.at[3]),
        pltpu.make_async_copy(acts_hbm, ACT, local_sems.at[4]),
    ]
    for load in loads:
        load.start()
    barrier = pltpu.get_barrier_semaphore()
    peers = [at(dy=d) for d in RING] + [at(dz=d) for d in (1, 2, 3)] + [at(dc=1), at(dy=2, dz=2)]
    peers += [at(dx=dx) for dx in (1, 2, 3)] + [flip(dx) for dx in (1, 2, 3)]
    for peer in peers:
        pl.semaphore_signal(barrier, inc=1, device_id=peer, device_id_type=MESH)

    loads[0].wait()
    own_up = UPOWN[...].reshape(2 * RANK, RANK)
    none = jnp.zeros_like(own_up)
    first_core = jnp.where(c == 0, 1.0, 0.0).astype(F32)
    UMINE[...] = (
        jnp.concatenate([own_up, none], axis=1) * first_core
        + jnp.concatenate([none, own_up], axis=1) * (1.0 - first_core)
    ).astype(BF16)
    loads[2].wait()
    for s in range(2):
        DT[dp * 2 + s] = DOWN[s].astype(BF16)
    pl.semaphore_wait(barrier, len(peers))
    start("u0", "d0")
    loads[1].wait()
    for j in range(4):
        inside = lax.broadcasted_iota(jnp.int32, (BLK, KEYS), 0) < left_ref[f * 4 + j]
        part = G[f, pl.ds(j * BLK, BLK)].astype(F32)
        G[f, pl.ds(j * BLK, BLK)] = jnp.where(inside, part, 0.0).astype(BF16)
    got("u0")
    mine, theirs = UMINE[pl.ds(c * RANK, RANK)], USIB[pl.ds(c * RANK, RANK)]
    UP[dp, c, :, pl.ds(pl.multiple_of(chip * 128, 128), 128)] = (
        mine.astype(F32) + theirs.astype(F32)
    ).astype(BF16)
    start(*[f"uy_{k}" for k in range(3)])
    got("d0")
    start(*[f"d1_{dx}_{l}" for dx in (1, 3, 2) for l in (0, 1)])
    got(*[f"uy_{k}" for k in range(3)])
    start(*[f"uz_{k}" for k in range(3)])
    start("yp0", "ym1", "yp1", "ym0", "c0")
    got(*[f"uz_{k}" for k in range(3)])
    start("zA0", "zA1", "zB")
    start(*[f"u2_{dx}_{l}" for dx in (1, 3, 2) for l in (0, 1)])
    loads[3].wait()
    WT[...] = BASE[...].T
    got(*[f"d1_{dx}_{l}" for dx in (1, 3, 2) for l in (0, 1)])
    loads[4].wait()

    def partial_low(fb):
        parts = []
        for j in range(4):
            block = ACT[pl.ds(fb * ROWS_OWN + j * BLK, BLK)]
            parts.append(
                lax.dot_general(DT[slot_ref[fb * 4 + j]], block, LAST, preferred_element_type=F32)
            )
        return jnp.concatenate(parts, axis=1)

    def low_step(q, _):
        LSIB[q] = partial_low(q * 2 + 1 - c).astype(BF16)
        LOWN[q] = partial_low(q * 2 + c)
        return 0

    lax.fori_loop(0, 8, low_step, 0)
    start("l0")
    got("zA0", "yp0", "ym1")
    got("l0")

    def sum_step(q, _):
        total = LOWN[q] + LGOT[q].astype(F32)
        LOWN[q] = total
        LSUM[q] = total.astype(BF16)
        return 0

    lax.fori_loop(0, 8, sum_step, 0)
    both = [f"{k}_{l}" for k in range(3) for l in (0, 1)]
    start(*["ly_" + k for k in both])

    got(*[f"u2_{dx}_{l}" for dx in (1, 3, 2) for l in (0, 1)])
    start("u3")
    got("zA1", "u3")
    for j in range(4):
        s = slot_ref[f * 4 + j]
        BK[chip, c, :, pl.ds(j * BLK, BLK)] = lax.dot_general(
            UP[s // 2, s % 2], G[f, pl.ds(j * BLK, BLK)], LAST, preferred_element_type=F32
        ).astype(BF16)
    start("bz", *[f"b_{k}_0" for k in range(3)])
    got("yp1")
    start("c1")
    got("ym0")
    start("c2")
    got("bz")
    start(*[f"b_{k}_1" for k in range(3)])
    start("fp", "fm")
    got(*["ly_" + k for k in both])
    total = LOWN[other]
    for k in range(3):
        total += LARR[k, 1].astype(F32)
    LZ[...] = total.astype(BF16)
    start("lz", "zBm")
    got("zB")
    start("c3")
    total = LOWN[chip]
    for k in range(3):
        total += LARR[k, 0].astype(F32)
    got("lz")
    LW[chip] = (total + LZARR[...].astype(F32)).astype(BF16)
    start("wz", *[f"w_{k}_0" for k in range(3)])
    start("zBp")
    got(*["b_" + k for k in both])
    start("b_c", "ap0", "am1")
    got("b_c")

    def spread(read, fb, at_column):
        for j in range(4):
            slot = slot_ref[fb * 4 + j]
            part = read(pl.ds(j * BLK, BLK)).astype(F32)
            for s in range(LANGS):
                weight = jnp.where(slot == s, 1.0, 0.0).astype(F32)
                EXP[pl.ds(s * RANK, RANK), pl.ds(at_column + j * BLK, BLK)] = (
                    part * weight
                ).astype(BF16)

    span = GROUP * ROWS_OWN

    def down_step(g, _):
        @pl.when(g == 16 // GROUP - 1)
        def _():
            got("wz")
            start(*[f"w_{k}_1" for k in range(3)])
            start("q", "ap1", "am0")

        for i in range(GROUP):
            fb = g * GROUP + i
            spread(lambda cols: BK[fb // 2, fb % 2, :, cols], fb, i * ROWS_OWN)
        part = jnp.dot(EXP[...], ACT[pl.ds(g * span, span)], preferred_element_type=F32)

        @pl.when(g == 0)
        def _():
            DG[...] = part

        @pl.when(g > 0)
        def _():
            DG[...] += part

        return 0

    lax.fori_loop(0, 16 // GROUP, down_step, 0)

    def scale_step(s, _):
        total = adapter_scale * DG[pl.ds(s * RANK, RANK)]
        DG[pl.ds(s * RANK, RANK)] = total
        DSEND[s] = total.astype(BF16)
        return 0

    lax.fori_loop(0, LANGS, scale_step, 0)
    start(*[f"r0_{k}_{l}" for k in range(3) for l in (0, 1)])
    got(*[f"w_{k}_0" for k in range(3)])
    got("fp", "fm")
    start("zB2", "c4")

    order = [(0, 0), (3, 0), (1, 0), (0, 1), (2, 0), (3, 1), (1, 1), (2, 1)]

    def write(fb, slot):
        return pltpu.make_async_copy(
            OB.at[slot], out_hbm.at[pl.ds(fb * ROWS_OWN, ROWS_OWN)], out_sems.at[slot]
        )

    def down_sum(l):
        total = DG[pl.ds((l * 4 + x) * 2 * RANK, 2 * RANK)]
        for k in range(3):
            total += DARR[k, l].astype(F32).reshape(2 * RANK, FEATURES)
        return total

    def main_step(t, _):
        i, core = t // 2, t % 2
        dy = jnp.int32(0)
        dh = jnp.int32(0)
        for k, (a, b) in enumerate(order):
            dy = jnp.where(i == k, a, dy)
            dh = jnp.where(i == k, b, dh)
        fb = chip_of(dy, dh) * 2 + lax.rem(c + core, 2)

        @pl.when(t == 1)
        def _():
            got("c0")

        @pl.when(t == 2)
        def _():
            got("ap0")
            start("fap")
            got("am1")
            start("fam")

        @pl.when(t == 3)
        def _():
            got("c1")

        @pl.when(t == 5)
        def _():
            got("c2")

        @pl.when(t == 6)
        def _():
            got(*[f"w_{k}_1" for k in range(3)])

        @pl.when(t == 7)
        def _():
            got("c3")

        @pl.when(t == 9)
        def _():
            got("c4")
            got(*[f"r0_{k}_{l}" for k in range(3) for l in (0, 1)])
            DZ[...] = down_sum(1 - zl).astype(BF16)
            start("r1")

        @pl.when(t == 10)
        def _():
            got("zBm", "ap1")
            start("c5")

        @pl.when(t == 11)
        def _():
            got("zBp", "am0")
            start("c6")
            got("c5")

        @pl.when(t == 13)
        def _():
            got("q")
            COLUMNS[...] = FAR[...]

        @pl.when(t == 14)
        def _():
            got("zB2")
            start("c7m")
            got("fap")
            start("c70")
            got("fam")
            start("c71")
            got("ux")
            USEND[...] += UHALF[...]
            start(*[f"v_{k}" for k in range(7)])

        @pl.when(t == 15)
        def _():
            got("r1")
            total = down_sum(zl) + DZARR[...].astype(F32)
            down_out[0] = total[:RANK]
            down_out[1] = total[RANK:]
            got("c7m", "c70", "c71")

        @pl.when((core == 0) & (t < 14))
        def _():
            COLUMNS[...] = G[fb, :, pl.ds(pl.multiple_of(chip * 128, 128), 128)]

        @pl.when(((core == 0) & (t < 14)) | (t == 13))
        def _():
            source = jnp.where(t == 13, chip_of(2, 1), fb // 2)
            spread(lambda cols: LW[source, :, cols], source * 2 + c, 0)
            part = jnp.dot(EXP[:, :ROWS_OWN], COLUMNS[...], preferred_element_type=F32)

            @pl.when(t == 0)
            def _():
                UG[...] = part

            @pl.when(t > 0)
            def _():
                UG[...] += part

        @pl.when(t == 13)
        def _():
            lane = lax.broadcasted_iota(jnp.int32, (RANK, 128), 1)
            for d in range(8):
                even = adapter_scale * UG[pl.ds(d * 2 * RANK, RANK)]
                odd = adapter_scale * UG[pl.ds(d * 2 * RANK + RANK, RANK)]
                left = jnp.where(lane < RANK, even, pltpu.roll(odd, RANK, 1))
                right = jnp.where(lane < RANK, pltpu.roll(even, RANK, 1), odd)
                USEND[d] = left * first_core + right * (1.0 - first_core)
                UOTHER[d] = right * first_core + left * (1.0 - first_core)
            start("ux")
            got("c6")

        slot = t % 2

        @pl.when(t >= 2)
        def _():
            write(fb, slot).wait()

        frozen = jnp.dot(G[fb], WT[...], preferred_element_type=F32)
        for j in range(4):
            low = lax.dot_general(
                BK[fb // 2, fb % 2, :, pl.ds(j * BLK, BLK)],
                DT[slot_ref[fb * 4 + j]],
                FIRST,
                preferred_element_type=F32,
            )
            OB[slot, pl.ds(j * BLK, BLK)] = (
                frozen[j * BLK : (j + 1) * BLK] + adapter_scale * low
            ).astype(BF16)
        write(fb, slot).start()
        return 0

    lax.fori_loop(0, 16, main_step, 0)
    got(*[f"v_{k}" for k in range(7)])
    total = USEND[dp]
    for k in range(7):
        total += UARR[k]
    up_out[...] = total
    write(f, 0).wait()
    write(f, 1).wait()
    for name in makers:
        makers[name]().wait_send()


def second_kernel(first_hbm, *refs):
    ins, out_hbm, outs = refs[:8], refs[8], refs[9:15]
    PIECES, scratch = refs[15], refs[16:30]
    in_sems, piece_in, piece_out, out_sems = refs[30:]
    loads = [
        pltpu.make_async_copy(ins[k], scratch[k], in_sems.at[k]) for k in range(8)
    ]
    pieces = [pl.ds(k * ROWS_OWN, ROWS_OWN) for k in range(16)]
    reads = [
        pltpu.make_async_copy(first_hbm.at[rows], PIECES.at[k], piece_in.at[k])
        for k, rows in enumerate(pieces)
    ]
    writes = [
        pltpu.make_async_copy(PIECES.at[k], out_hbm.at[rows], piece_out.at[k])
        for k, rows in enumerate(pieces)
    ]
    for copy in (*reads[:4], *loads, *reads[4:]):
        copy.start()
    for k in range(4):
        reads[k].wait()
        writes[k].start()
    for copy in loads:
        copy.wait()
    down_grad, up_grad, down, down_first, down_second, up, up_first, up_second = scratch[:8]
    results = scratch[8:]
    for ref, value in zip(
        results[:3], adam_update(down[...], down_first[...], down_second[...], down_grad[...])
    ):
        ref[...] = value
    both = up_grad[...]
    for s, gradient in enumerate((both[:, :RANK], pltpu.roll(both, RANK, 1)[:, :RANK])):
        for ref, value in zip(results[3:], adam_update(up[s], up_first[s], up_second[s], gradient)):
            ref[s] = value
    stores = [pltpu.make_async_copy(results[k], outs[k], out_sems.at[k]) for k in range(6)]
    for copy in stores:
        copy.start()
    for k in range(4, 16):
        reads[k].wait()
        writes[k].start()
    for copy in (*writes, *stores):
        copy.wait()


def on_device(
    activations,
    grad_out,
    base_weight,
    down_param,
    up_param,
    down_first,
    down_second,
    up_first,
    up_second,
    counts,
    slot_language,
):
    slots, left = block_layout(counts, slot_language, lax.axis_index("dp") * BLOCKS_DP)
    smem = pl.BlockSpec(memory_space=pltpu.SMEM)
    anywhere = pl.BlockSpec(memory_space=pl.ANY)
    vmem = pl.BlockSpec(memory_space=pltpu.VMEM)
    n_messages = 120
    first_out, down_own, up_own = pl.pallas_call(
        kernel,
        out_shape=(
            jax.ShapeDtypeStruct(activations.shape, BF16),
            jax.ShapeDtypeStruct((2, RANK, FEATURES), F32),
            jax.ShapeDtypeStruct((RANK, 128), F32),
        ),
        in_specs=[smem, smem] + [anywhere] * 5,
        out_specs=(anywhere, vmem, vmem),
        scratch_shapes=[
            pltpu.VMEM((16, ROWS_OWN, KEYS), BF16),
            pltpu.VMEM((16 * ROWS_OWN, FEATURES), BF16),
            pltpu.VMEM((FEATURES, KEYS), BF16),
            pltpu.VMEM((KEYS, FEATURES), BF16),
            pltpu.VMEM((2, RANK, FEATURES), F32),
            pltpu.VMEM((2, RANK, RANK), F32),
            pltpu.VMEM((8, 2, RANK, KEYS), BF16),
            pltpu.VMEM((2 * RANK, 128), BF16),
            pltpu.VMEM((2 * RANK, 128), BF16),
            pltpu.VMEM((LANGS, RANK, FEATURES), BF16),
            pltpu.VMEM((8, 2, RANK, ROWS_OWN), BF16),
            pltpu.VMEM((8, RANK, ROWS_OWN), BF16),
            pltpu.VMEM((8, RANK, ROWS_OWN), F32),
            pltpu.VMEM((8, RANK, ROWS_OWN), BF16),
            pltpu.VMEM((8, RANK, ROWS_OWN), BF16),
            pltpu.VMEM((8, RANK, ROWS_OWN), BF16),
            pltpu.VMEM((3, 2, RANK, ROWS_OWN), BF16),
            pltpu.VMEM((RANK, ROWS_OWN), BF16),
            pltpu.VMEM((RANK, ROWS_OWN), BF16),
            pltpu.VMEM((LANGS * RANK, FEATURES), F32),
            pltpu.VMEM((LANGS, RANK, FEATURES), BF16),
            pltpu.VMEM((3, 2, 2, RANK, FEATURES), BF16),
            pltpu.VMEM((2 * RANK, FEATURES), BF16),
            pltpu.VMEM((2 * RANK, FEATURES), BF16),
            pltpu.VMEM((LANGS * RANK, 128), F32),
            pltpu.VMEM((ROWS_OWN, 128), BF16),
            pltpu.VMEM((ROWS_OWN, 128), BF16),
            pltpu.VMEM((8, RANK, 128), F32),
            pltpu.VMEM((8, RANK, 128), F32),
            pltpu.VMEM((8, RANK, 128), F32),
            pltpu.VMEM((7, RANK, 128), F32),
            pltpu.VMEM((LANGS * RANK, GROUP * ROWS_OWN), BF16),
            pltpu.VMEM((2, ROWS_OWN, FEATURES), BF16),
            pltpu.SemaphoreType.DMA((n_messages,)),
            pltpu.SemaphoreType.DMA((n_messages,)),
            pltpu.SemaphoreType.DMA((5,)),
            pltpu.SemaphoreType.DMA((2,)),
        ],
        compiler_params=pltpu.CompilerParams(
            collective_id=0, has_side_effects=True, vmem_limit_bytes=58 * 2**20
        ),
        cost_estimate=pl.CostEstimate(
            flops=2 * 8192 * 512 * 1024 * 3, bytes_accessed=40 * 2**20, transcendentals=0
        ),
    )(slots, left, activations, grad_out, base_weight, turn(down_param), up_param)
    down_shape, up_shape = (2, RANK, FEATURES), (2, RANK, RANK)
    shapes = [down_shape] * 3 + [up_shape] * 3
    input_gradient, new_down, new_down_first, new_down_second, new_up, new_up_first, new_up_second = (
        pl.pallas_call(
            second_kernel,
            out_shape=[jax.ShapeDtypeStruct(activations.shape, BF16)]
            + [jax.ShapeDtypeStruct(shape, F32) for shape in shapes],
            in_specs=[anywhere] * 9,
            out_specs=[anywhere] * 7,
            scratch_shapes=[pltpu.VMEM((16, ROWS_OWN, FEATURES), BF16)]
            + [pltpu.VMEM(shape, F32) for shape in [down_shape, (RANK, 128)] + shapes + shapes]
            + [pltpu.SemaphoreType.DMA((k,)) for k in (8, 16, 16, 6)],
            compiler_params=pltpu.CompilerParams(vmem_limit_bytes=60 * 2**20),
            cost_estimate=pl.CostEstimate(
                flops=2**20, bytes_accessed=20 * 2**20, transcendentals=0
            ),
        )(
            first_out, down_own, up_own,
            turn(down_param), turn(down_first), turn(down_second), up_param, up_first, up_second,
        )
    )
    new_down, new_down_first, new_down_second = map(
        turn, (new_down, new_down_first, new_down_second)
    )
    return (
        input_gradient,
        new_down,
        new_up,
        new_down_first,
        new_down_second,
        new_up_first,
        new_up_second,
    )


def solution(mesh):
    placed = (
        P("dp", "fsdp"),
        P(("dp", "fsdp"), None),
        P("fsdp", None),
        P("dp", "fsdp", None),
        P("dp", None, "fsdp"),
        P("dp", "fsdp", None),
        P("dp", "fsdp", None),
        P("dp", None, "fsdp"),
        P("dp", None, "fsdp"),
        P(),
        P(),
    )
    return jax.shard_map(
        on_device,
        mesh=mesh,
        in_specs=placed,
        out_specs=(
            P("dp", "fsdp"),
            P("dp", "fsdp", None),
            P("dp", None, "fsdp"),
            P("dp", "fsdp", None),
            P("dp", "fsdp", None),
            P("dp", None, "fsdp"),
            P("dp", None, "fsdp"),
        ),
        check_vma=False,
    )
```

```python
import jax
import jax.numpy as jnp
from jax import lax
from jax.experimental import pallas as pl
from jax.experimental.pallas import tpu as pltpu
from jax.sharding import PartitionSpec as P

BLK = 128
STEP = 100
BLOCKS_DP = 64
LANGS = 16
RANK = 64
ROWS_OWN = 512
GROUP = 4
FEATURES = 512
KEYS = 1024

adapter_scale = 2.0
beta_first = 0.9
beta_second = 0.999
learn_rate = 0.001
adam_epsilon = 1e-08

MESH = pl.DeviceIdType.MESH
F32 = jnp.float32
BF16 = jnp.bfloat16
LAST = (((1,), (1,)), ((), ()))
FIRST = (((0,), (0,)), ((), ()))
CUT = 128
RING = (1, 3, 2)
DATA = [(dx, dl) for dl in range(2) for dx in range(4) if (dx, dl) != (0, 0)]


def adam_update(param, first, second, gradient):
    new_first = beta_first * first + (1.0 - beta_first) * gradient
    new_second = beta_second * second + (1.0 - beta_second) * gradient * gradient
    first_hat = new_first / (1.0 - beta_first**STEP)
    second_hat = new_second / (1.0 - beta_second**STEP)
    new_param = param - learn_rate * first_hat / (jnp.sqrt(second_hat) + adam_epsilon)
    return (new_param, new_first, new_second)


def turn(a):
    return jnp.swapaxes(a, 1, 2)


def kernel(
    count_ref, language_ref, acts_hbm, grad_hbm, base_hbm, down_hbm, up_hbm,
    out_hbm, down_out, up_out,
    G, ACT, BASE, WT, DOWN, UPOWN, UP, UMINE, USIB, DT, BK, LW, LOWN, LSIB, LGOT, LSUM, LARR, LZ, LZARR,
    DG, DSEND, DARR, DZ, DZARR, UG, FAR, COLUMNS, UOTHER, UHALF, USEND, UARR, EXP, OB, send_sems, recv_sems, local_sems, out_sems,
    language_start, slot_start, slot_count, slot_ref,
):
    dp, f = lax.axis_index("dp"), lax.axis_index("fsdp")
    x, zl = lax.rem(dp, 4), dp // 4
    c, chip = lax.rem(f, 2), f // 2
    y, h = lax.rem(chip, 4), chip // 4
    z = h * 2 + zl

    def at(dx=0, dy=0, dz=0, dc=0):
        zz = lax.rem(z + dz, 4)
        return (
            lax.rem(zz, 2) * 4 + lax.rem(x + dx, 4),
            (zz // 2) * 8 + lax.rem(y + dy, 4) * 2 + lax.rem(c + dc, 2),
        )

    def flip(dx):
        return ((1 - zl) * 4 + lax.rem(x + dx, 4), f)

    def chip_of(dy, dh):
        return lax.rem(h + dh, 2) * 4 + lax.rem(y + dy, 4)

    makers = {}

    def message(name, src, dst, device):
        k = len(makers)
        makers[name] = lambda: pltpu.make_async_remote_copy(
            src_ref=src(),
            dst_ref=dst(),
            send_sem=send_sems.at[k],
            recv_sem=recv_sems.at[k],
            device_id=device(),
            device_id_type=MESH,
        )

    def same(name, ref, device):
        message(name, ref, ref, device)

    def start(*names):
        for name in names:
            makers[name]().start()

    def got(*names):
        for name in names:
            makers[name]().wait_recv()

    def rows(name, by, bh, lo, hi, **to):
        same(name, lambda: G.at[chip_of(by, bh) * 2 + c, pl.ds(lo, hi - lo)], lambda: at(**to))

    top, low_end, n = CUT, ROWS_OWN - CUT, ROWS_OWN
    half = n // 2
    plus, minus, across, sibling = dict(dy=1), dict(dy=3), dict(dz=2), dict(dc=1)
    rows("yp0", 0, 0, 0, half, **plus)
    rows("ym1", 0, 0, half, n, **minus)
    rows("zA0", 0, 0, 0, top, **across)
    rows("zA1", 0, 0, low_end, n, **across)
    rows("yp1", 0, 0, half, n, **plus)
    rows("ym0", 0, 0, 0, half, **minus)
    rows("zB", 0, 0, top, low_end, **across)
    rows("c0", 0, 0, 0, n, **sibling)
    rows("ap0", 0, 1, 0, top, **plus)
    rows("am0", 0, 1, 0, top, **minus)
    rows("ap1", 0, 1, low_end, n, **plus)
    rows("am1", 0, 1, low_end, n, **minus)
    rows("fp", 3, 0, 0, half, **plus)
    rows("fm", 1, 0, half, n, **minus)
    rows("zBm", 3, 0, top, low_end, **across)
    rows("zBp", 1, 0, top, low_end, **across)
    rows("c1", 3, 0, 0, n, **sibling)
    rows("c2", 1, 0, 0, n, **sibling)
    rows("c3", 0, 1, 0, n, **sibling)
    rows("fap", 3, 1, 0, top, **plus)
    rows("fam", 1, 1, low_end, n, **minus)
    rows("zB2", 2, 0, top, low_end, **across)
    rows("c4", 2, 0, 0, n, **sibling)
    rows("c5", 3, 1, 0, n, **sibling)
    rows("c6", 1, 1, 0, n, **sibling)
    rows("c7m", 2, 1, top, low_end, **sibling)
    rows("c70", 2, 1, 0, top, **sibling)
    rows("c71", 2, 1, low_end, n, **sibling)
    message("u0", lambda: UMINE, lambda: USIB, lambda: at(dc=1))
    for k, dy in enumerate(RING):
        same(
            f"uy_{k}",
            lambda: UP.at[dp, c, :, pl.ds(pl.multiple_of(chip * 128, 128), 128)],
            lambda dy=dy: at(dy=dy),
        )
    for k, dz in enumerate((1, 3, 2)):
        same(
            f"uz_{k}",
            lambda: UP.at[dp, c, :, pl.ds(pl.multiple_of(h * 512, 128), 512)],
            lambda dz=dz: at(dz=dz),
        )
    message(
        "q",
        lambda: G.at[f, :, pl.ds(pl.multiple_of(chip_of(2, 1) * 128, 128), 128)],
        lambda: FAR,
        lambda: at(dy=2, dz=2),
    )
    for dx in (1, 3):
        for l in (0, 1):
            same(f"u2_{dx}_{l}", lambda l=l: UP.at[l * 4 + x, c], lambda dx=dx: at(dx=dx))
    same("u2_f1", lambda: UP.at[lax.rem(x + 3, 4), c], lambda: at(dx=1))
    same("u2_f3", lambda: UP.at[4 + lax.rem(x + 1, 4), c], lambda: at(dx=3))
    same("u3", lambda: UP.at[:, c], lambda: at(dc=1))
    same("d0", lambda: DT.at[pl.ds(dp * 2, 2)], lambda: flip(0))
    same("d1_f1", lambda: DT.at[pl.ds(lax.rem(x + 3, 4) * 2, 2)], lambda: at(dx=1))
    same("d1_f3", lambda: DT.at[pl.ds((4 + lax.rem(x + 1, 4)) * 2, 2)], lambda: at(dx=3))
    for dx in (1, 3):
        for l in (0, 1):
            same(
                f"d1_{dx}_{l}",
                lambda l=l: DT.at[pl.ds((l * 4 + x) * 2, 2)],
                lambda dx=dx: at(dx=dx),
            )
    other = chip_of(0, 1)
    for k, dy in enumerate(RING):
        to = lambda dy=dy: at(dy=dy)
        for l in (0, 1):
            message(
                f"ly_{k}_{l}",
                lambda dy=dy, l=l: LSUM.at[chip_of(dy, l)],
                lambda k=k, l=l: LARR.at[k, l],
                to,
            )
            same(f"b_{k}_{l}", lambda l=l: BK.at[chip_of(0, l), c], to)
            same(f"w_{k}_{l}", lambda l=l: LW.at[chip_of(0, l)], to)
    message("lz", lambda: LZ, lambda: LZARR, lambda: at(dz=2))
    same("bz", lambda: BK.at[chip, c], lambda: at(dz=2))
    same("wz", lambda: LW.at[chip], lambda: at(dz=2))
    message("ux", lambda: UOTHER, lambda: UHALF, lambda: at(dc=1))
    same("b_c", lambda: BK.at[:, c], lambda: at(dc=1))
    message("l0", lambda: LSIB, lambda: LGOT, lambda: at(dc=1))
    for k, dx in enumerate((1, 3, 2)):
        for l in (0, 1):
            message(
                f"r0_{k}_{l}",
                lambda dx=dx, l=l: DSEND.at[pl.ds((l * 4 + lax.rem(x + dx, 4)) * 2, 2)],
                lambda k=k, l=l: DARR.at[k, l],
                lambda dx=dx: at(dx=dx),
            )
    message("r1", lambda: DZ, lambda: DZARR, lambda: flip(0))
    for k, (dx, dl) in enumerate(DATA):
        message(
            f"v_{k}",
            lambda dx=dx, dl=dl: USEND.at[lax.rem(zl + dl, 2) * 4 + lax.rem(x + dx, 4)],
            lambda k=k: UARR.at[k],
            lambda dx=dx, dl=dl: (lax.rem(zl + dl, 2) * 4 + lax.rem(x + dx, 4), f),
        )

    loads = [
        pltpu.make_async_copy(up_hbm, UPOWN, local_sems.at[0]),
        pltpu.make_async_copy(grad_hbm, G.at[f], local_sems.at[1]),
        pltpu.make_async_copy(down_hbm, DOWN, local_sems.at[2]),
        pltpu.make_async_copy(base_hbm, BASE, local_sems.at[3]),
        pltpu.make_async_copy(acts_hbm, ACT, local_sems.at[4]),
    ]
    for load in loads:
        load.start()
    barrier = pltpu.get_barrier_semaphore()
    peers = [at(dy=d) for d in RING] + [at(dz=d) for d in (1, 2, 3)] + [at(dc=1), at(dy=2, dz=2)]
    peers += [at(dx=dx) for dx in (1, 2, 3)] + [flip(dx) for dx in (1, 2, 3)]
    for peer in peers:
        pl.semaphore_signal(barrier, inc=1, device_id=peer, device_id_type=MESH)

    running = jnp.int32(0)
    for l in range(LANGS):
        language_start[l] = running
        running += (count_ref[l] + BLK - 1) // BLK
    for s in range(LANGS):
        slot_start[s] = language_start[language_ref[s]]
        slot_count[s] = count_ref[language_ref[s]]

    def layout(b):
        slot, live = jnp.int32(0), jnp.int32(0)
        for s in range(LANGS):
            behind = dp * BLOCKS_DP + b - slot_start[s]
            left = slot_count[s] - behind * BLK
            hot = (behind >= 0) & (left > 0)
            slot, live = jnp.where(hot, s, slot), jnp.where(hot, left, live)
        return slot, live

    live_rows = [layout(f * 4 + j)[1] for j in range(4)]

    loads[0].wait()
    own_up = UPOWN[...].reshape(2 * RANK, RANK)
    none = jnp.zeros_like(own_up)
    first_core = jnp.where(c == 0, 1.0, 0.0).astype(F32)
    UMINE[...] = (
        jnp.concatenate([own_up, none], axis=1) * first_core
        + jnp.concatenate([none, own_up], axis=1) * (1.0 - first_core)
    ).astype(BF16)
    loads[2].wait()
    for s in range(2):
        DT[dp * 2 + s] = DOWN[s].astype(BF16)
    pl.semaphore_wait(barrier, len(peers))
    start("u0", "d0")
    loads[1].wait()
    for j in range(4):
        inside = lax.broadcasted_iota(jnp.int32, (BLK, KEYS), 0) < live_rows[j]
        part = G[f, pl.ds(j * BLK, BLK)].astype(F32)
        G[f, pl.ds(j * BLK, BLK)] = jnp.where(inside, part, 0.0).astype(BF16)
    got("u0")
    mine, theirs = UMINE[pl.ds(c * RANK, RANK)], USIB[pl.ds(c * RANK, RANK)]
    UP[dp, c, :, pl.ds(pl.multiple_of(chip * 128, 128), 128)] = (
        mine.astype(F32) + theirs.astype(F32)
    ).astype(BF16)
    start(*[f"uy_{k}" for k in range(3)])
    got("d0")
    start(*[f"d1_{dx}_{l}" for l in (0, 1) for dx in (1, 3)])
    got(*[f"uy_{k}" for k in range(3)])
    start(*[f"uz_{k}" for k in range(3)])
    start("yp0", "ym1", "yp1", "ym0", "c0")
    got(*[f"uz_{k}" for k in range(3)])
    start("zA0", "zA1", "zB")
    start(*[f"u2_{dx}_{l}" for l in (0, 1) for dx in (1, 3)])

    def slot_step(b, _):
        slot_ref[b] = layout(b)[0]
        return 0

    lax.fori_loop(0, BLOCKS_DP, slot_step, 0)
    loads[3].wait()
    WT[...] = BASE[...].T
    got("d1_1_0")
    start("d1_f1")
    got("d1_3_1")
    start("d1_f3")
    got("d1_1_1", "d1_3_0")
    got("u2_1_0")
    start("u2_f1")
    got("u2_3_1")
    start("u2_f3")
    got("d1_f1", "d1_f3")
    loads[4].wait()

    def partial_low(fb):
        parts = []
        for j in range(4):
            block = ACT[pl.ds(fb * ROWS_OWN + j * BLK, BLK)]
            parts.append(
                lax.dot_general(DT[slot_ref[fb * 4 + j]], block, LAST, preferred_element_type=F32)
            )
        return jnp.concatenate(parts, axis=1)

    def low_step(q, _):
        LSIB[q] = partial_low(q * 2 + 1 - c).astype(BF16)
        LOWN[q] = partial_low(q * 2 + c)
        return 0

    lax.fori_loop(0, 8, low_step, 0)
    start("l0")
    got("u2_1_1", "u2_3_0", "u2_f1", "u2_f3")
    start("u3")
    got("zA0", "yp0", "ym1")
    got("l0")

    def sum_step(q, _):
        total = LOWN[q] + LGOT[q].astype(F32)
        LOWN[q] = total
        LSUM[q] = total.astype(BF16)
        return 0

    lax.fori_loop(0, 8, sum_step, 0)
    both = [f"{k}_{l}" for k in range(3) for l in (0, 1)]
    start(*["ly_" + k for k in both])

    got("zA1", "u3")
    for j in range(4):
        s = slot_ref[f * 4 + j]
        BK[chip, c, :, pl.ds(j * BLK, BLK)] = lax.dot_general(
            UP[s // 2, s % 2], G[f, pl.ds(j * BLK, BLK)], LAST, preferred_element_type=F32
        ).astype(BF16)
    start("bz", *[f"b_{k}_0" for k in range(3)])
    got("yp1")
    start("c1")
    got("ym0")
    start("c2")
    got("bz")
    start(*[f"b_{k}_1" for k in range(3)])
    start("fp", "fm")
    got(*["ly_" + k for k in both])
    total = LOWN[other]
    for k in range(3):
        total += LARR[k, 1].astype(F32)
    LZ[...] = total.astype(BF16)
    start("lz", "zBm")
    got("zB")
    start("c3")
    total = LOWN[chip]
    for k in range(3):
        total += LARR[k, 0].astype(F32)
    got("lz")
    LW[chip] = (total + LZARR[...].astype(F32)).astype(BF16)
    start("wz", *[f"w_{k}_0" for k in range(3)])
    start("zBp")
    got(*["b_" + k for k in both])
    start("b_c", "ap0", "am1")
    got("b_c")

    def spread(read, fb, at_column):
        for j in range(4):
            slot = slot_ref[fb * 4 + j]
            part = read(pl.ds(j * BLK, BLK)).astype(F32)
            for s in range(LANGS):
                weight = jnp.where(slot == s, 1.0, 0.0).astype(F32)
                EXP[pl.ds(s * RANK, RANK), pl.ds(at_column + j * BLK, BLK)] = (
                    part * weight
                ).astype(BF16)

    span = GROUP * ROWS_OWN

    def down_step(g, _):
        @pl.when(g == 16 // GROUP - 1)
        def _():
            got("wz")
            start(*[f"w_{k}_1" for k in range(3)])
            start("q", "ap1", "am0")

        for i in range(GROUP):
            fb = g * GROUP + i
            spread(lambda cols: BK[fb // 2, fb % 2, :, cols], fb, i * ROWS_OWN)
        part = jnp.dot(EXP[...], ACT[pl.ds(g * span, span)], preferred_element_type=F32)

        @pl.when(g == 0)
        def _():
            DG[...] = part

        @pl.when(g > 0)
        def _():
            DG[...] += part

        return 0

    lax.fori_loop(0, 16 // GROUP, down_step, 0)

    def scale_step(s, _):
        total = adapter_scale * DG[pl.ds(s * RANK, RANK)]
        DG[pl.ds(s * RANK, RANK)] = total
        DSEND[s] = total.astype(BF16)
        return 0

    lax.fori_loop(0, LANGS, scale_step, 0)
    start(*[f"r0_{k}_{l}" for k in range(3) for l in (0, 1)])
    got(*[f"w_{k}_0" for k in range(3)])
    got("fp", "fm")
    start("zB2", "c4")

    order = [(0, 0), (3, 0), (1, 0), (0, 1), (2, 0), (3, 1), (1, 1), (2, 1)]

    def write(fb, slot):
        return pltpu.make_async_copy(
            OB.at[slot], out_hbm.at[pl.ds(fb * ROWS_OWN, ROWS_OWN)], out_sems.at[slot]
        )

    def down_sum(l):
        total = DG[pl.ds((l * 4 + x) * 2 * RANK, 2 * RANK)]
        for k in range(3):
            total += DARR[k, l].astype(F32).reshape(2 * RANK, FEATURES)
        return total

    def main_step(t, _):
        i, core = t // 2, t % 2
        dy = jnp.int32(0)
        dh = jnp.int32(0)
        for k, (a, b) in enumerate(order):
            dy = jnp.where(i == k, a, dy)
            dh = jnp.where(i == k, b, dh)
        fb = chip_of(dy, dh) * 2 + lax.rem(c + core, 2)

        @pl.when(t == 1)
        def _():
            got("c0")

        @pl.when(t == 2)
        def _():
            got("ap0")
            start("fap")
            got("am1")
            start("fam")

        @pl.when(t == 3)
        def _():
            got("c1")

        @pl.when(t == 5)
        def _():
            got("c2")

        @pl.when(t == 6)
        def _():
            got(*[f"w_{k}_1" for k in range(3)])

        @pl.when(t == 7)
        def _():
            got("c3")

        @pl.when(t == 9)
        def _():
            got("c4")
            got(*[f"r0_{k}_{l}" for k in range(3) for l in (0, 1)])
            DZ[...] = down_sum(1 - zl).astype(BF16)
            start("r1")

        @pl.when(t == 10)
        def _():
            got("zBm", "ap1")
            start("c5")

        @pl.when(t == 11)
        def _():
            got("zBp", "am0")
            start("c6")
            got("c5")

        @pl.when(t == 13)
        def _():
            got("q")
            COLUMNS[...] = FAR[...]

        @pl.when(t == 14)
        def _():
            got("zB2")
            start("c7m")
            got("fap")
            start("c70")
            got("fam")
            start("c71")
            got("ux")
            USEND[...] += UHALF[...]
            start(*[f"v_{k}" for k in range(7)])

        @pl.when(t == 15)
        def _():
            got("r1")
            total = down_sum(zl) + DZARR[...].astype(F32)
            down_out[0] = total[:RANK]
            down_out[1] = total[RANK:]
            got("c7m", "c70", "c71")

        @pl.when((core == 0) & (t < 14))
        def _():
            COLUMNS[...] = G[fb, :, pl.ds(pl.multiple_of(chip * 128, 128), 128)]

        @pl.when(((core == 0) & (t < 14)) | (t == 13))
        def _():
            source = jnp.where(t == 13, chip_of(2, 1), fb // 2)
            spread(lambda cols: LW[source, :, cols], source * 2 + c, 0)
            part = jnp.dot(EXP[:, :ROWS_OWN], COLUMNS[...], preferred_element_type=F32)

            @pl.when(t == 0)
            def _():
                UG[...] = part

            @pl.when(t > 0)
            def _():
                UG[...] += part

        @pl.when(t == 13)
        def _():
            lane = lax.broadcasted_iota(jnp.int32, (RANK, 128), 1)
            for d in range(8):
                even = adapter_scale * UG[pl.ds(d * 2 * RANK, RANK)]
                odd = adapter_scale * UG[pl.ds(d * 2 * RANK + RANK, RANK)]
                left = jnp.where(lane < RANK, even, pltpu.roll(odd, RANK, 1))
                right = jnp.where(lane < RANK, pltpu.roll(even, RANK, 1), odd)
                USEND[d] = left * first_core + right * (1.0 - first_core)
                UOTHER[d] = right * first_core + left * (1.0 - first_core)
            start("ux")
            got("c6")

        slot = t % 2

        @pl.when(t >= 2)
        def _():
            write(fb, slot).wait()

        frozen = jnp.dot(G[fb], WT[...], preferred_element_type=F32)
        for j in range(4):
            low = lax.dot_general(
                BK[fb // 2, fb % 2, :, pl.ds(j * BLK, BLK)],
                DT[slot_ref[fb * 4 + j]],
                FIRST,
                preferred_element_type=F32,
            )
            OB[slot, pl.ds(j * BLK, BLK)] = (
                frozen[j * BLK : (j + 1) * BLK] + adapter_scale * low
            ).astype(BF16)
        write(fb, slot).start()
        return 0

    lax.fori_loop(0, 16, main_step, 0)
    got(*[f"v_{k}" for k in range(7)])
    total = USEND[dp]
    for k in range(7):
        total += UARR[k]
    up_out[...] = total
    write(f, 0).wait()
    write(f, 1).wait()
    for name in makers:
        makers[name]().wait_send()


def second_kernel(first_hbm, *refs):
    ins, out_hbm, outs = refs[:8], refs[8], refs[9:15]
    PIECES, scratch = refs[15], refs[16:30]
    in_sems, piece_in, piece_out, out_sems = refs[30:]
    loads = [
        pltpu.make_async_copy(ins[k], scratch[k], in_sems.at[k]) for k in range(8)
    ]
    pieces = [pl.ds(k * ROWS_OWN, ROWS_OWN) for k in range(16)]
    reads = [
        pltpu.make_async_copy(first_hbm.at[rows], PIECES.at[k], piece_in.at[k])
        for k, rows in enumerate(pieces)
    ]
    writes = [
        pltpu.make_async_copy(PIECES.at[k], out_hbm.at[rows], piece_out.at[k])
        for k, rows in enumerate(pieces)
    ]
    for copy in (*reads[:4], *loads, *reads[4:]):
        copy.start()
    for k in range(4):
        reads[k].wait()
        writes[k].start()
    for copy in loads:
        copy.wait()
    down_grad, up_grad, down, down_first, down_second, up, up_first, up_second = scratch[:8]
    results = scratch[8:]
    for ref, value in zip(
        results[:3], adam_update(down[...], down_first[...], down_second[...], down_grad[...])
    ):
        ref[...] = value
    both = up_grad[...]
    for s, gradient in enumerate((both[:, :RANK], pltpu.roll(both, RANK, 1)[:, :RANK])):
        for ref, value in zip(results[3:], adam_update(up[s], up_first[s], up_second[s], gradient)):
            ref[s] = value
    stores = [pltpu.make_async_copy(results[k], outs[k], out_sems.at[k]) for k in range(6)]
    for copy in stores:
        copy.start()
    for k in range(4, 16):
        reads[k].wait()
        writes[k].start()
    for copy in (*writes, *stores):
        copy.wait()


def on_device(
    activations,
    grad_out,
    base_weight,
    down_param,
    up_param,
    down_first,
    down_second,
    up_first,
    up_second,
    counts,
    slot_language,
):
    smem = pl.BlockSpec(memory_space=pltpu.SMEM)
    anywhere = pl.BlockSpec(memory_space=pl.ANY)
    vmem = pl.BlockSpec(memory_space=pltpu.VMEM)
    n_messages = 120
    first_out, down_own, up_own = pl.pallas_call(
        kernel,
        out_shape=(
            jax.ShapeDtypeStruct(activations.shape, BF16),
            jax.ShapeDtypeStruct((2, RANK, FEATURES), F32),
            jax.ShapeDtypeStruct((RANK, 128), F32),
        ),
        in_specs=[smem, smem] + [anywhere] * 5,
        out_specs=(anywhere, vmem, vmem),
        scratch_shapes=[
            pltpu.VMEM((16, ROWS_OWN, KEYS), BF16),
            pltpu.VMEM((16 * ROWS_OWN, FEATURES), BF16),
            pltpu.VMEM((FEATURES, KEYS), BF16),
            pltpu.VMEM((KEYS, FEATURES), BF16),
            pltpu.VMEM((2, RANK, FEATURES), F32),
            pltpu.VMEM((2, RANK, RANK), F32),
            pltpu.VMEM((8, 2, RANK, KEYS), BF16),
            pltpu.VMEM((2 * RANK, 128), BF16),
            pltpu.VMEM((2 * RANK, 128), BF16),
            pltpu.VMEM((LANGS, RANK, FEATURES), BF16),
            pltpu.VMEM((8, 2, RANK, ROWS_OWN), BF16),
            pltpu.VMEM((8, RANK, ROWS_OWN), BF16),
            pltpu.VMEM((8, RANK, ROWS_OWN), F32),
            pltpu.VMEM((8, RANK, ROWS_OWN), BF16),
            pltpu.VMEM((8, RANK, ROWS_OWN), BF16),
            pltpu.VMEM((8, RANK, ROWS_OWN), BF16),
            pltpu.VMEM((3, 2, RANK, ROWS_OWN), BF16),
            pltpu.VMEM((RANK, ROWS_OWN), BF16),
            pltpu.VMEM((RANK, ROWS_OWN), BF16),
            pltpu.VMEM((LANGS * RANK, FEATURES), F32),
            pltpu.VMEM((LANGS, RANK, FEATURES), BF16),
            pltpu.VMEM((3, 2, 2, RANK, FEATURES), BF16),
            pltpu.VMEM((2 * RANK, FEATURES), BF16),
            pltpu.VMEM((2 * RANK, FEATURES), BF16),
            pltpu.VMEM((LANGS * RANK, 128), F32),
            pltpu.VMEM((ROWS_OWN, 128), BF16),
            pltpu.VMEM((ROWS_OWN, 128), BF16),
            pltpu.VMEM((8, RANK, 128), F32),
            pltpu.VMEM((8, RANK, 128), F32),
            pltpu.VMEM((8, RANK, 128), F32),
            pltpu.VMEM((7, RANK, 128), F32),
            pltpu.VMEM((LANGS * RANK, GROUP * ROWS_OWN), BF16),
            pltpu.VMEM((2, ROWS_OWN, FEATURES), BF16),
            pltpu.SemaphoreType.DMA((n_messages,)),
            pltpu.SemaphoreType.DMA((n_messages,)),
            pltpu.SemaphoreType.DMA((5,)),
            pltpu.SemaphoreType.DMA((2,)),
            pltpu.SMEM((LANGS,), jnp.int32),
            pltpu.SMEM((LANGS,), jnp.int32),
            pltpu.SMEM((LANGS,), jnp.int32),
            pltpu.SMEM((BLOCKS_DP,), jnp.int32),
        ],
        compiler_params=pltpu.CompilerParams(
            collective_id=0, has_side_effects=True, vmem_limit_bytes=58 * 2**20
        ),
        cost_estimate=pl.CostEstimate(
            flops=2 * 8192 * 512 * 1024 * 3, bytes_accessed=40 * 2**20, transcendentals=0
        ),
    )(counts, slot_language, activations, grad_out, base_weight, turn(down_param), up_param)
    down_shape, up_shape = (2, RANK, FEATURES), (2, RANK, RANK)
    shapes = [down_shape] * 3 + [up_shape] * 3
    input_gradient, new_down, new_down_first, new_down_second, new_up, new_up_first, new_up_second = (
        pl.pallas_call(
            second_kernel,
            out_shape=[jax.ShapeDtypeStruct(activations.shape, BF16)]
            + [jax.ShapeDtypeStruct(shape, F32) for shape in shapes],
            in_specs=[anywhere] * 9,
            out_specs=[anywhere] * 7,
            scratch_shapes=[pltpu.VMEM((16, ROWS_OWN, FEATURES), BF16)]
            + [pltpu.VMEM(shape, F32) for shape in [down_shape, (RANK, 128)] + shapes + shapes]
            + [pltpu.SemaphoreType.DMA((k,)) for k in (8, 16, 16, 6)],
            compiler_params=pltpu.CompilerParams(vmem_limit_bytes=60 * 2**20),
            cost_estimate=pl.CostEstimate(
                flops=2**20, bytes_accessed=20 * 2**20, transcendentals=0
            ),
        )(
            first_out, down_own, up_own,
            turn(down_param), turn(down_first), turn(down_second), up_param, up_first, up_second,
        )
    )
    new_down, new_down_first, new_down_second = map(
        turn, (new_down, new_down_first, new_down_second)
    )
    return (
        input_gradient,
        new_down,
        new_up,
        new_down_first,
        new_down_second,
        new_up_first,
        new_up_second,
    )


def solution(mesh):
    placed = (
        P("dp", "fsdp"),
        P(("dp", "fsdp"), None),
        P("fsdp", None),
        P("dp", "fsdp", None),
        P("dp", None, "fsdp"),
        P("dp", "fsdp", None),
        P("dp", "fsdp", None),
        P("dp", None, "fsdp"),
        P("dp", None, "fsdp"),
        P(),
        P(),
    )
    return jax.shard_map(
        on_device,
        mesh=mesh,
        in_specs=placed,
        out_specs=(
            P("dp", "fsdp"),
            P("dp", "fsdp", None),
            P("dp", None, "fsdp"),
            P("dp", "fsdp", None),
            P("dp", "fsdp", None),
            P("dp", None, "fsdp"),
            P("dp", None, "fsdp"),
        ),
        check_vma=False,
    )
```

```python
import jax
import jax.numpy as jnp
from jax import lax
from jax.experimental import pallas as pl
from jax.experimental.pallas import tpu as pltpu
from jax.sharding import PartitionSpec as P

BLK = 128
STEP = 100
BLOCKS_DP = 64
LANGS = 16
RANK = 64
ROWS_OWN = 512
GROUP = 4
FEATURES = 512
KEYS = 1024

adapter_scale = 2.0
beta_first = 0.9
beta_second = 0.999
learn_rate = 0.001
adam_epsilon = 1e-08

MESH = pl.DeviceIdType.MESH
F32 = jnp.float32
BF16 = jnp.bfloat16
LAST = (((1,), (1,)), ((), ()))
FIRST = (((0,), (0,)), ((), ()))
CUT = 128
RING = (1, 3, 2)
DATA = [(dx, dl) for dl in range(2) for dx in range(4) if (dx, dl) != (0, 0)]


def adam_update(param, first, second, gradient):
    new_first = beta_first * first + (1.0 - beta_first) * gradient
    new_second = beta_second * second + (1.0 - beta_second) * gradient * gradient
    first_hat = new_first / (1.0 - beta_first**STEP)
    second_hat = new_second / (1.0 - beta_second**STEP)
    new_param = param - learn_rate * first_hat / (jnp.sqrt(second_hat) + adam_epsilon)
    return (new_param, new_first, new_second)


def turn(a):
    return jnp.swapaxes(a, 1, 2)


def kernel(
    count_ref, language_ref, acts_hbm, grad_hbm, base_hbm, down_hbm, up_hbm,
    out_hbm, down_out, up_out,
    G, ACT, BASE, WT, DOWN, UPOWN, UP, UMINE, USIB, DT, BK, LW, LOWN, LSIB, LGOT, LSUM, LARR, LZ, LZARR,
    DG, DSEND, DARR, DZ, DZARR, UG, FAR, COLUMNS, UOTHER, UHALF, USEND, UARR, EXP, OB, send_sems, recv_sems, local_sems, out_sems,
    language_start, slot_start, slot_count, slot_ref,
):
    dp, f = lax.axis_index("dp"), lax.axis_index("fsdp")
    x, zl = lax.rem(dp, 4), dp // 4
    c, chip = lax.rem(f, 2), f // 2
    y, h = lax.rem(chip, 4), chip // 4
    z = h * 2 + zl

    def at(dx=0, dy=0, dz=0, dc=0):
        zz = lax.rem(z + dz, 4)
        return (
            lax.rem(zz, 2) * 4 + lax.rem(x + dx, 4),
            (zz // 2) * 8 + lax.rem(y + dy, 4) * 2 + lax.rem(c + dc, 2),
        )

    def flip(dx):
        return ((1 - zl) * 4 + lax.rem(x + dx, 4), f)

    def chip_of(dy, dh):
        return lax.rem(h + dh, 2) * 4 + lax.rem(y + dy, 4)

    makers = {}

    def message(name, src, dst, device):
        k = len(makers)
        makers[name] = lambda: pltpu.make_async_remote_copy(
            src_ref=src(),
            dst_ref=dst(),
            send_sem=send_sems.at[k],
            recv_sem=recv_sems.at[k],
            device_id=device(),
            device_id_type=MESH,
        )

    def same(name, ref, device):
        message(name, ref, ref, device)

    def start(*names):
        for name in names:
            makers[name]().start()

    def got(*names):
        for name in names:
            makers[name]().wait_recv()

    def rows(name, by, bh, lo, hi, **to):
        same(name, lambda: G.at[chip_of(by, bh) * 2 + c, pl.ds(lo, hi - lo)], lambda: at(**to))

    top, low_end, n = CUT, ROWS_OWN - CUT, ROWS_OWN
    half = n // 2
    plus, minus, across, sibling = dict(dy=1), dict(dy=3), dict(dz=2), dict(dc=1)
    rows("yp0", 0, 0, 0, half, **plus)
    rows("ym1", 0, 0, half, n, **minus)
    rows("zA0", 0, 0, 0, top, **across)
    rows("zA1", 0, 0, low_end, n, **across)
    rows("yp1", 0, 0, half, n, **plus)
    rows("ym0", 0, 0, 0, half, **minus)
    rows("zB", 0, 0, top, low_end, **across)
    rows("c0", 0, 0, 0, n, **sibling)
    rows("ap0", 0, 1, 0, top, **plus)
    rows("am0", 0, 1, 0, top, **minus)
    rows("ap1", 0, 1, low_end, n, **plus)
    rows("am1", 0, 1, low_end, n, **minus)
    rows("fp", 3, 0, 0, half, **plus)
    rows("fm", 1, 0, half, n, **minus)
    rows("zBm", 3, 0, top, low_end, **across)
    rows("zBp", 1, 0, top, low_end, **across)
    rows("c1", 3, 0, 0, n, **sibling)
    rows("c2", 1, 0, 0, n, **sibling)
    rows("c3", 0, 1, 0, n, **sibling)
    rows("fap", 3, 1, 0, top, **plus)
    rows("fam", 1, 1, low_end, n, **minus)
    rows("zB2", 2, 0, top, low_end, **across)
    rows("c4", 2, 0, 0, n, **sibling)
    rows("c5", 3, 1, 0, n, **sibling)
    rows("c6", 1, 1, 0, n, **sibling)
    rows("c7m", 2, 1, top, low_end, **sibling)
    rows("c70", 2, 1, 0, top, **sibling)
    rows("c71", 2, 1, low_end, n, **sibling)
    message("u0", lambda: UMINE, lambda: USIB, lambda: at(dc=1))
    for k, dy in enumerate(RING):
        same(
            f"uy_{k}",
            lambda: UP.at[dp, c, :, pl.ds(pl.multiple_of(chip * 128, 128), 128)],
            lambda dy=dy: at(dy=dy),
        )
    for k, dz in enumerate((1, 3, 2)):
        same(
            f"uz_{k}",
            lambda: UP.at[dp, c, :, pl.ds(pl.multiple_of(h * 512, 128), 512)],
            lambda dz=dz: at(dz=dz),
        )
    message(
        "q",
        lambda: G.at[f, :, pl.ds(pl.multiple_of(chip_of(2, 1) * 128, 128), 128)],
        lambda: FAR,
        lambda: at(dy=2, dz=2),
    )
    for dx in (1, 3):
        for l in (0, 1):
            same(f"u2_{dx}_{l}", lambda l=l: UP.at[l * 4 + x, c], lambda dx=dx: at(dx=dx))
    same("u2_f1", lambda: UP.at[lax.rem(x + 3, 4), c], lambda: at(dx=1))
    same("u2_f3", lambda: UP.at[4 + lax.rem(x + 1, 4), c], lambda: at(dx=3))
    same("u3", lambda: UP.at[:, c], lambda: at(dc=1))
    same("d0", lambda: DT.at[pl.ds(dp * 2, 2)], lambda: flip(0))
    same("d1_f1", lambda: DT.at[pl.ds(lax.rem(x + 3, 4) * 2, 2)], lambda: at(dx=1))
    same("d1_f3", lambda: DT.at[pl.ds((4 + lax.rem(x + 1, 4)) * 2, 2)], lambda: at(dx=3))
    for dx in (1, 3):
        for l in (0, 1):
            same(
                f"d1_{dx}_{l}",
                lambda l=l: DT.at[pl.ds((l * 4 + x) * 2, 2)],
                lambda dx=dx: at(dx=dx),
            )
    other = chip_of(0, 1)
    for k, dy in enumerate(RING):
        to = lambda dy=dy: at(dy=dy)
        for l in (0, 1):
            message(
                f"ly_{k}_{l}",
                lambda dy=dy, l=l: LSUM.at[chip_of(dy, l)],
                lambda k=k, l=l: LARR.at[k, l],
                to,
            )
            same(f"b_{k}_{l}", lambda l=l: BK.at[chip_of(0, l), c], to)
            same(f"w_{k}_{l}", lambda l=l: LW.at[chip_of(0, l)], to)
    message("lz", lambda: LZ, lambda: LZARR, lambda: at(dz=2))
    same("bz", lambda: BK.at[chip, c], lambda: at(dz=2))
    same("wz", lambda: LW.at[chip], lambda: at(dz=2))
    message("ux", lambda: UOTHER, lambda: UHALF, lambda: at(dc=1))
    same("b_c", lambda: BK.at[:, c], lambda: at(dc=1))
    message("l0", lambda: LSIB, lambda: LGOT, lambda: at(dc=1))
    for k, dx in enumerate((1, 3, 2)):
        for l in (0, 1):
            message(
                f"r0_{k}_{l}",
                lambda dx=dx, l=l: DSEND.at[pl.ds((l * 4 + lax.rem(x + dx, 4)) * 2, 2)],
                lambda k=k, l=l: DARR.at[k, l],
                lambda dx=dx: at(dx=dx),
            )
    message("r1", lambda: DZ, lambda: DZARR, lambda: flip(0))
    for k, (dx, dl) in enumerate(DATA):
        message(
            f"v_{k}",
            lambda dx=dx, dl=dl: USEND.at[lax.rem(zl + dl, 2) * 4 + lax.rem(x + dx, 4)],
            lambda k=k: UARR.at[k],
            lambda dx=dx, dl=dl: (lax.rem(zl + dl, 2) * 4 + lax.rem(x + dx, 4), f),
        )

    loads = [
        pltpu.make_async_copy(up_hbm, UPOWN, local_sems.at[0]),
        pltpu.make_async_copy(grad_hbm, G.at[f], local_sems.at[1]),
        pltpu.make_async_copy(down_hbm, DOWN, local_sems.at[2]),
        pltpu.make_async_copy(base_hbm, BASE, local_sems.at[3]),
        pltpu.make_async_copy(acts_hbm, ACT, local_sems.at[4]),
    ]
    for load in loads:
        load.start()
    barrier = pltpu.get_barrier_semaphore()
    peers = [at(dy=d) for d in RING] + [at(dz=d) for d in (1, 2, 3)] + [at(dc=1), at(dy=2, dz=2)]
    peers += [at(dx=dx) for dx in (1, 2, 3)] + [flip(dx) for dx in (1, 2, 3)]
    for peer in peers:
        pl.semaphore_signal(barrier, inc=1, device_id=peer, device_id_type=MESH)

    running = jnp.int32(0)
    for l in range(LANGS):
        language_start[l] = running
        running += (count_ref[l] + BLK - 1) // BLK
    for s in range(LANGS):
        slot_start[s] = language_start[language_ref[s]]
        slot_count[s] = count_ref[language_ref[s]]

    def layout(b):
        slot, live = jnp.int32(0), jnp.int32(0)
        for s in range(LANGS):
            behind = dp * BLOCKS_DP + b - slot_start[s]
            left = slot_count[s] - behind * BLK
            hot = (behind >= 0) & (left > 0)
            slot, live = jnp.where(hot, s, slot), jnp.where(hot, left, live)
        return slot, live

    live_rows = [layout(f * 4 + j)[1] for j in range(4)]

    loads[0].wait()
    own_up = UPOWN[...].reshape(2 * RANK, RANK)
    none = jnp.zeros_like(own_up)
    first_core = jnp.where(c == 0, 1.0, 0.0).astype(F32)
    UMINE[...] = (
        jnp.concatenate([own_up, none], axis=1) * first_core
        + jnp.concatenate([none, own_up], axis=1) * (1.0 - first_core)
    ).astype(BF16)
    loads[2].wait()
    for s in range(2):
        DT[dp * 2 + s] = DOWN[s].astype(BF16)
    pl.semaphore_wait(barrier, len(peers))
    start("u0", "d0")
    loads[1].wait()
    for j in range(4):
        inside = lax.broadcasted_iota(jnp.int32, (BLK, KEYS), 0) < live_rows[j]
        part = G[f, pl.ds(j * BLK, BLK)].astype(F32)
        G[f, pl.ds(j * BLK, BLK)] = jnp.where(inside, part, 0.0).astype(BF16)
    got("u0")
    mine, theirs = UMINE[pl.ds(c * RANK, RANK)], USIB[pl.ds(c * RANK, RANK)]
    UP[dp, c, :, pl.ds(pl.multiple_of(chip * 128, 128), 128)] = (
        mine.astype(F32) + theirs.astype(F32)
    ).astype(BF16)
    start(*[f"uy_{k}" for k in range(3)])
    got("d0")
    start(*[f"d1_{dx}_{l}" for l in (0, 1) for dx in (1, 3)])
    got(*[f"uy_{k}" for k in range(3)])
    start(*[f"uz_{k}" for k in range(3)])
    start("yp0", "ym1", "yp1", "ym0", "c0")
    got(*[f"uz_{k}" for k in range(3)])
    start("zA0", "zA1", "zB")
    start(*[f"u2_{dx}_{l}" for l in (0, 1) for dx in (1, 3)])

    def slot_step(b, _):
        slot_ref[b] = layout(b)[0]
        return 0

    lax.fori_loop(0, BLOCKS_DP, slot_step, 0)
    loads[3].wait()
    WT[...] = BASE[...].T
    got("d1_1_0")
    start("d1_f1")
    got("d1_3_1")
    start("d1_f3")
    got("d1_1_1", "d1_3_0")
    got("u2_1_0")
    start("u2_f1")
    got("u2_3_1")
    start("u2_f3")
    got("d1_f1", "d1_f3")
    loads[4].wait()

    def partial_low(fb):
        parts = []
        for j in range(4):
            block = ACT[pl.ds(fb * ROWS_OWN + j * BLK, BLK)]
            parts.append(
                lax.dot_general(DT[slot_ref[fb * 4 + j]], block, LAST, preferred_element_type=F32)
            )
        return jnp.concatenate(parts, axis=1)

    def low_step(q, _):
        LSIB[q] = partial_low(q * 2 + 1 - c).astype(BF16)
        LOWN[q] = partial_low(q * 2 + c)
        return 0

    lax.fori_loop(0, 8, low_step, 0)
    start("l0")
    got("u2_1_1", "u2_3_0", "u2_f1", "u2_f3")
    start("u3")
    got("zA0", "yp0", "ym1")
    got("l0")

    def sum_step(q, _):
        total = LOWN[q] + LGOT[q].astype(F32)
        LOWN[q] = total
        LSUM[q] = total.astype(BF16)
        return 0

    lax.fori_loop(0, 8, sum_step, 0)
    both = [f"{k}_{l}" for k in range(3) for l in (0, 1)]
    start(*["ly_" + k for k in both])

    got("zA1", "u3")
    for j in range(4):
        s = slot_ref[f * 4 + j]
        BK[chip, c, :, pl.ds(j * BLK, BLK)] = lax.dot_general(
            UP[s // 2, s % 2], G[f, pl.ds(j * BLK, BLK)], LAST, preferred_element_type=F32
        ).astype(BF16)
    start("bz", *[f"b_{k}_0" for k in range(3)])
    got("yp1")
    start("c1")
    got("ym0")
    start("c2")
    got("bz")
    start(*[f"b_{k}_1" for k in range(3)])
    start("fp", "fm")
    got(*["ly_" + k for k in both])
    total = LOWN[other]
    for k in range(3):
        total += LARR[k, 1].astype(F32)
    LZ[...] = total.astype(BF16)
    start("lz", "zBm")
    got("zB")
    start("c3")
    total = LOWN[chip]
    for k in range(3):
        total += LARR[k, 0].astype(F32)
    got("lz")
    LW[chip] = (total + LZARR[...].astype(F32)).astype(BF16)
    start("wz", *[f"w_{k}_0" for k in range(3)])
    start("zBp")
    got(*["b_" + k for k in both])
    start("b_c", "ap0", "am1")
    got("b_c")

    def spread(read, fb, at_column):
        for j in range(4):
            slot = slot_ref[fb * 4 + j]
            part = read(pl.ds(j * BLK, BLK)).astype(F32)
            for s in range(LANGS):
                weight = jnp.where(slot == s, 1.0, 0.0).astype(F32)
                EXP[pl.ds(s * RANK, RANK), pl.ds(at_column + j * BLK, BLK)] = (
                    part * weight
                ).astype(BF16)

    span = GROUP * ROWS_OWN

    def down_step(g, _):
        @pl.when(g == 16 // GROUP - 1)
        def _():
            got("wz")
            start(*[f"w_{k}_1" for k in range(3)])
            start("q", "ap1", "am0")

        for i in range(GROUP):
            fb = g * GROUP + i
            spread(lambda cols: BK[fb // 2, fb % 2, :, cols], fb, i * ROWS_OWN)
        part = jnp.dot(EXP[...], ACT[pl.ds(g * span, span)], preferred_element_type=F32)

        @pl.when(g == 0)
        def _():
            DG[...] = part

        @pl.when(g > 0)
        def _():
            DG[...] += part

        return 0

    lax.fori_loop(0, 16 // GROUP, down_step, 0)

    def scale_step(s, _):
        total = adapter_scale * DG[pl.ds(s * RANK, RANK)]
        DG[pl.ds(s * RANK, RANK)] = total
        DSEND[s] = total.astype(BF16)
        return 0

    lax.fori_loop(0, LANGS, scale_step, 0)
    start(*[f"r0_{k}_{l}" for k in range(3) for l in (0, 1)])
    got(*[f"w_{k}_0" for k in range(3)])
    got("fp", "fm")
    start("zB2", "c4")

    order = [(0, 0), (3, 0), (1, 0), (0, 1), (2, 0), (3, 1), (1, 1), (2, 1)]

    def write(fb, slot):
        return pltpu.make_async_copy(
            OB.at[slot], out_hbm.at[pl.ds(fb * ROWS_OWN, ROWS_OWN)], out_sems.at[slot]
        )

    def down_sum(l):
        total = DG[pl.ds((l * 4 + x) * 2 * RANK, 2 * RANK)]
        for k in range(3):
            total += DARR[k, l].astype(F32).reshape(2 * RANK, FEATURES)
        return total

    def main_step(t, _):
        i, core = t // 2, t % 2
        dy = jnp.int32(0)
        dh = jnp.int32(0)
        for k, (a, b) in enumerate(order):
            dy = jnp.where(i == k, a, dy)
            dh = jnp.where(i == k, b, dh)
        fb = chip_of(dy, dh) * 2 + lax.rem(c + core, 2)

        @pl.when(t == 1)
        def _():
            got("c0")

        @pl.when(t == 2)
        def _():
            got("ap0")
            start("fap")
            got("am1")
            start("fam")

        @pl.when(t == 3)
        def _():
            got("c1")

        @pl.when(t == 5)
        def _():
            got("c2")

        @pl.when(t == 6)
        def _():
            got(*[f"w_{k}_1" for k in range(3)])

        @pl.when(t == 7)
        def _():
            got("c3")

        @pl.when(t == 9)
        def _():
            got("c4")

        @pl.when(t == 12)
        def _():
            got(*[f"r0_{k}_{l}" for k in range(3) for l in (0, 1)])
            DZ[...] = down_sum(1 - zl).astype(BF16)
            start("r1")

        @pl.when(t == 10)
        def _():
            got("zBm", "ap1")
            start("c5")

        @pl.when(t == 11)
        def _():
            got("zBp", "am0")
            start("c6")
            got("c5")

        @pl.when(t == 13)
        def _():
            got("q")
            COLUMNS[...] = FAR[...]

        @pl.when(t == 14)
        def _():
            got("zB2")
            start("c7m")
            got("fap")
            start("c70")
            got("fam")
            start("c71")
            got("ux")
            USEND[...] += UHALF[...]
            start(*[f"v_{k}" for k in range(7)])

        @pl.when(t == 15)
        def _():
            got("r1")
            total = down_sum(zl) + DZARR[...].astype(F32)
            down_out[0] = total[:RANK]
            down_out[1] = total[RANK:]
            got("c7m", "c70", "c71")

        @pl.when((core == 0) & (t < 14))
        def _():
            COLUMNS[...] = G[fb, :, pl.ds(pl.multiple_of(chip * 128, 128), 128)]

        @pl.when(((core == 0) & (t < 14)) | (t == 13))
        def _():
            source = jnp.where(t == 13, chip_of(2, 1), fb // 2)
            spread(lambda cols: LW[source, :, cols], source * 2 + c, 0)
            part = jnp.dot(EXP[:, :ROWS_OWN], COLUMNS[...], preferred_element_type=F32)

            @pl.when(t == 0)
            def _():
                UG[...] = part

            @pl.when(t > 0)
            def _():
                UG[...] += part

        @pl.when(t == 13)
        def _():
            lane = lax.broadcasted_iota(jnp.int32, (RANK, 128), 1)
            for d in range(8):
                even = adapter_scale * UG[pl.ds(d * 2 * RANK, RANK)]
                odd = adapter_scale * UG[pl.ds(d * 2 * RANK + RANK, RANK)]
                left = jnp.where(lane < RANK, even, pltpu.roll(odd, RANK, 1))
                right = jnp.where(lane < RANK, pltpu.roll(even, RANK, 1), odd)
                USEND[d] = left * first_core + right * (1.0 - first_core)
                UOTHER[d] = right * first_core + left * (1.0 - first_core)
            start("ux")
            got("c6")

        slot = t % 2

        @pl.when(t >= 2)
        def _():
            write(fb, slot).wait()

        frozen = jnp.dot(G[fb], WT[...], preferred_element_type=F32)
        for j in range(4):
            low = lax.dot_general(
                BK[fb // 2, fb % 2, :, pl.ds(j * BLK, BLK)],
                DT[slot_ref[fb * 4 + j]],
                FIRST,
                preferred_element_type=F32,
            )
            OB[slot, pl.ds(j * BLK, BLK)] = (
                frozen[j * BLK : (j + 1) * BLK] + adapter_scale * low
            ).astype(BF16)
        write(fb, slot).start()
        return 0

    lax.fori_loop(0, 16, main_step, 0)
    got(*[f"v_{k}" for k in range(7)])
    total = USEND[dp]
    for k in range(7):
        total += UARR[k]
    up_out[...] = total
    write(f, 0).wait()
    write(f, 1).wait()
    for name in makers:
        makers[name]().wait_send()


def second_kernel(first_hbm, *refs):
    ins, out_hbm, outs = refs[:8], refs[8], refs[9:15]
    PIECES, scratch = refs[15], refs[16:30]
    in_sems, piece_in, piece_out, out_sems = refs[30:]
    loads = [
        pltpu.make_async_copy(ins[k], scratch[k], in_sems.at[k]) for k in range(8)
    ]
    pieces = [pl.ds(k * ROWS_OWN, ROWS_OWN) for k in range(16)]
    reads = [
        pltpu.make_async_copy(first_hbm.at[rows], PIECES.at[k], piece_in.at[k])
        for k, rows in enumerate(pieces)
    ]
    writes = [
        pltpu.make_async_copy(PIECES.at[k], out_hbm.at[rows], piece_out.at[k])
        for k, rows in enumerate(pieces)
    ]
    for copy in (*reads[:8], *loads, *reads[8:]):
        copy.start()
    for k in range(12):
        reads[k].wait()
        writes[k].start()
    for copy in loads:
        copy.wait()
    down_grad, up_grad, down, down_first, down_second, up, up_first, up_second = scratch[:8]
    results = scratch[8:]
    for ref, value in zip(
        results[:3], adam_update(down[...], down_first[...], down_second[...], down_grad[...])
    ):
        ref[...] = value
    both = up_grad[...]
    for s, gradient in enumerate((both[:, :RANK], pltpu.roll(both, RANK, 1)[:, :RANK])):
        for ref, value in zip(results[3:], adam_update(up[s], up_first[s], up_second[s], gradient)):
            ref[s] = value
    stores = [pltpu.make_async_copy(results[k], outs[k], out_sems.at[k]) for k in range(6)]
    for copy in stores:
        copy.start()
    for k in range(12, 16):
        reads[k].wait()
        writes[k].start()
    for copy in (*writes, *stores):
        copy.wait()


def on_device(
    activations,
    grad_out,
    base_weight,
    down_param,
    up_param,
    down_first,
    down_second,
    up_first,
    up_second,
    counts,
    slot_language,
):
    smem = pl.BlockSpec(memory_space=pltpu.SMEM)
    anywhere = pl.BlockSpec(memory_space=pl.ANY)
    vmem = pl.BlockSpec(memory_space=pltpu.VMEM)
    n_messages = 120
    first_out, down_own, up_own = pl.pallas_call(
        kernel,
        out_shape=(
            jax.ShapeDtypeStruct(activations.shape, BF16),
            jax.ShapeDtypeStruct((2, RANK, FEATURES), F32),
            jax.ShapeDtypeStruct((RANK, 128), F32),
        ),
        in_specs=[smem, smem] + [anywhere] * 5,
        out_specs=(anywhere, vmem, vmem),
        scratch_shapes=[
            pltpu.VMEM((16, ROWS_OWN, KEYS), BF16),
            pltpu.VMEM((16 * ROWS_OWN, FEATURES), BF16),
            pltpu.VMEM((FEATURES, KEYS), BF16),
            pltpu.VMEM((KEYS, FEATURES), BF16),
            pltpu.VMEM((2, RANK, FEATURES), F32),
            pltpu.VMEM((2, RANK, RANK), F32),
            pltpu.VMEM((8, 2, RANK, KEYS), BF16),
            pltpu.VMEM((2 * RANK, 128), BF16),
            pltpu.VMEM((2 * RANK, 128), BF16),
            pltpu.VMEM((LANGS, RANK, FEATURES), BF16),
            pltpu.VMEM((8, 2, RANK, ROWS_OWN), BF16),
            pltpu.VMEM((8, RANK, ROWS_OWN), BF16),
            pltpu.VMEM((8, RANK, ROWS_OWN), F32),
            pltpu.VMEM((8, RANK, ROWS_OWN), BF16),
            pltpu.VMEM((8, RANK, ROWS_OWN), BF16),
            pltpu.VMEM((8, RANK, ROWS_OWN), BF16),
            pltpu.VMEM((3, 2, RANK, ROWS_OWN), BF16),
            pltpu.VMEM((RANK, ROWS_OWN), BF16),
            pltpu.VMEM((RANK, ROWS_OWN), BF16),
            pltpu.VMEM((LANGS * RANK, FEATURES), F32),
            pltpu.VMEM((LANGS, RANK, FEATURES), BF16),
            pltpu.VMEM((3, 2, 2, RANK, FEATURES), BF16),
            pltpu.VMEM((2 * RANK, FEATURES), BF16),
            pltpu.VMEM((2 * RANK, FEATURES), BF16),
            pltpu.VMEM((LANGS * RANK, 128), F32),
            pltpu.VMEM((ROWS_OWN, 128), BF16),
            pltpu.VMEM((ROWS_OWN, 128), BF16),
            pltpu.VMEM((8, RANK, 128), F32),
            pltpu.VMEM((8, RANK, 128), F32),
            pltpu.VMEM((8, RANK, 128), F32),
            pltpu.VMEM((7, RANK, 128), F32),
            pltpu.VMEM((LANGS * RANK, GROUP * ROWS_OWN), BF16),
            pltpu.VMEM((2, ROWS_OWN, FEATURES), BF16),
            pltpu.SemaphoreType.DMA((n_messages,)),
            pltpu.SemaphoreType.DMA((n_messages,)),
            pltpu.SemaphoreType.DMA((5,)),
            pltpu.SemaphoreType.DMA((2,)),
            pltpu.SMEM((LANGS,), jnp.int32),
            pltpu.SMEM((LANGS,), jnp.int32),
            pltpu.SMEM((LANGS,), jnp.int32),
            pltpu.SMEM((BLOCKS_DP,), jnp.int32),
        ],
        compiler_params=pltpu.CompilerParams(
            collective_id=0, has_side_effects=True, vmem_limit_bytes=58 * 2**20
        ),
        cost_estimate=pl.CostEstimate(
            flops=2 * 8192 * 512 * 1024 * 3, bytes_accessed=40 * 2**20, transcendentals=0
        ),
    )(counts, slot_language, activations, grad_out, base_weight, turn(down_param), up_param)
    down_shape, up_shape = (2, RANK, FEATURES), (2, RANK, RANK)
    shapes = [down_shape] * 3 + [up_shape] * 3
    input_gradient, new_down, new_down_first, new_down_second, new_up, new_up_first, new_up_second = (
        pl.pallas_call(
            second_kernel,
            out_shape=[jax.ShapeDtypeStruct(activations.shape, BF16)]
            + [jax.ShapeDtypeStruct(shape, F32) for shape in shapes],
            in_specs=[anywhere] * 9,
            out_specs=[anywhere] * 7,
            scratch_shapes=[pltpu.VMEM((16, ROWS_OWN, FEATURES), BF16)]
            + [pltpu.VMEM(shape, F32) for shape in [down_shape, (RANK, 128)] + shapes + shapes]
            + [pltpu.SemaphoreType.DMA((k,)) for k in (8, 16, 16, 6)],
            compiler_params=pltpu.CompilerParams(vmem_limit_bytes=60 * 2**20),
            cost_estimate=pl.CostEstimate(
                flops=2**20, bytes_accessed=20 * 2**20, transcendentals=0
            ),
        )(
            first_out, down_own, up_own,
            turn(down_param), turn(down_first), turn(down_second), up_param, up_first, up_second,
        )
    )
    new_down, new_down_first, new_down_second = map(
        turn, (new_down, new_down_first, new_down_second)
    )
    return (
        input_gradient,
        new_down,
        new_up,
        new_down_first,
        new_down_second,
        new_up_first,
        new_up_second,
    )


def solution(mesh):
    placed = (
        P("dp", "fsdp"),
        P(("dp", "fsdp"), None),
        P("fsdp", None),
        P("dp", "fsdp", None),
        P("dp", None, "fsdp"),
        P("dp", "fsdp", None),
        P("dp", "fsdp", None),
        P("dp", None, "fsdp"),
        P("dp", None, "fsdp"),
        P(),
        P(),
    )
    return jax.shard_map(
        on_device,
        mesh=mesh,
        in_specs=placed,
        out_specs=(
            P("dp", "fsdp"),
            P("dp", "fsdp", None),
            P("dp", None, "fsdp"),
            P("dp", "fsdp", None),
            P("dp", "fsdp", None),
            P("dp", None, "fsdp"),
            P("dp", None, "fsdp"),
        ),
        check_vma=False,
    )
```
